128 devices in a mesh: box: 32 (over y, z, core), sx: 2 (over x_lo), sy: 2 (over x_hi).
Axes of the slice: x: 4 (x_hi: 2, x_lo: 2; x = x_hi * 2 + x_lo), y: 4, z: 4, core: 2. Of those that a mesh axis runs over, the one named last changes fastest.
Arguments:
- coarse: float32 [256, 96, 128], P('box'), may hold values from -4 to 4
- anchors: int32 [32, 3], replicated, may hold values from 0 to 234, as said below
- dielectric: float32 [32, 80, 64, 256], P('box', 'sx', 'sy'), may hold values from 0.5 to 4
- screening: float32 [32, 80, 64, 256], P('box', 'sx', 'sy'), may hold values from 0.2 to 2
- source: float32 [32, 80, 64, 256], P('box', 'sx', 'sy'), may hold values from -40 to 40
Outputs:
- potential: float32 [32, 80, 64, 256], P('box', 'sx', 'sy')
- box_norm: float32 [32], P('box')
The draws below stay inside these ranges and needn't reach their ends.
Inputs may be any that keep to these rules, and one draw needn't show every extreme that they name: `anchors`: column 0 of each row is at most 234, column 1 at most 78, column 2 at most 62; some box reaches all three of these, and some box begins at coarse cell 0 in every dimension.
All inputs are finite; a program needn't handle non-finite values.
Results may differ from the reference program's by a relative error of at most 0.000098.
Values sent between devices are 32-bit elements; how exact they have to be, the bound alone decides.
A program may use at most 128 MiB of HBM per device.

```python
import math
import jax
import jax.numpy as jnp
from jax import lax

FZ = 256
GY = 96
GZ = 128
RATIO = 4
SWEEPS = 2
BOXES = 32
FX = 80
FY = 64
GX = 256
CBX = 22
CBY = 18
CBZ = 66


def draw_anchors(key, part):
    key = jax.random.fold_in(key, 3)
    value_key, order_key = jax.random.split(key)
    limits = jnp.array([GX - CBX + 1, GY - CBY + 1, GZ - CBZ + 1], dtype=jnp.int32)
    values = jax.random.randint(value_key, (BOXES, 3), 0, limits[None, :], dtype=jnp.int32)
    order = jax.random.permutation(order_key, BOXES)
    row_ids = jnp.arange(BOXES, dtype=jnp.int32)[:, None]
    values = jnp.where(row_ids == order[0], (limits - 1)[None, :], values)
    values = jnp.where(row_ids == order[1], jnp.zeros_like(values), values)
    return values.astype(jnp.int32)


def draw_source(key, part):
    key = jax.random.fold_in(key, 7)
    value_key, plane_key = jax.random.split(key)
    ramp_x = 1.0 + 3.0 * jnp.arange(FX, dtype=jnp.float32) / FX
    ramp_y = 1.0 + 3.0 * jnp.arange(FY, dtype=jnp.float32) / FY
    plane = jnp.exp(jax.random.uniform(plane_key, (BOXES, 1, 1, FZ), jnp.float32) * 2.302585)
    values = jnp.clip(jax.random.normal(value_key, (BOXES, FX, FY, FZ), jnp.float32), -4.0, 4.0)
    return 0.06 * values * ramp_x[None, :, None, None] * ramp_y[None, None, :, None] * plane


def steps_of(key, shape, shards, smallest, top_value):
    def one(axis_at, parts):
        steps = jax.random.uniform(jax.random.fold_in(jax.random.fold_in(key, 6), axis_at), (parts,), jnp.float32, smallest / len(shards), top_value / len(shards))
        return jnp.repeat(jnp.exp(steps), shape[axis_at] // parts).reshape((-1,) + (1,) * (len(shape) - axis_at - 1))

    loudness = one(*shards[0])
    for cut in shards[1:]:
        loudness = loudness * one(*cut)
    return loudness


def scatter_about(key, shape, scale, bound, cuts=(), held_as=jnp.bfloat16):
    drawn = jax.random.normal(key, shape, jnp.float32) * scale
    if len(cuts) > 0:
        drawn = steps_of(key, shape, cuts, -0.22, 0.18) * drawn
    return jnp.clip(drawn, min=-bound, max=bound).astype(held_as)


def setup_inputs(seed: int = 0) -> dict:
    key_of = jax.random.split(jax.random.key(seed), 6)
    coarse = scatter_about(key_of[0], (GX, GY, GZ), 1.0, 4.0, ((0, 32),), jnp.float32)
    anchors = draw_anchors(jax.random.fold_in(key_of[5], 71), 0)
    dielectric = jnp.clip(jnp.exp(math.log(4.0) - 2.0794415 * jax.random.uniform(key_of[2], (BOXES, FX, FY, FZ), jnp.float32) ** steps_of(key_of[2], (BOXES, FX, FY, FZ), ((0, 32), (1, 2), (2, 2)), -0.2, 0.2)), 0.5, 4.0)
    screening = jnp.clip(jnp.exp(math.log(2.0) - 2.3025851 * jax.random.uniform(key_of[3], (BOXES, FX, FY, FZ), jnp.float32) ** steps_of(key_of[3], (BOXES, FX, FY, FZ), ((0, 32), (1, 2), (2, 2)), -0.2, 0.2)), 0.2, 2.0)
    source = draw_source(jax.random.fold_in(key_of[5], 71), 0)
    return {"coarse": coarse, "anchors": anchors, "dielectric": dielectric, "screening": screening, "source": source}


def spread(leading, amount, extent):
    fine_index = leading + jnp.arange(amount, dtype=jnp.int32)
    shifted = fine_index + 1
    lower = jnp.clip(shifted // RATIO, 0, extent - 2)
    fraction = jnp.clip((shifted - lower * RATIO).astype(jnp.float32) / RATIO, 0.0, 1.0)
    columns = jnp.arange(extent, dtype=jnp.int32)[None, :]
    below = jnp.where(columns == lower[:, None], 1.0 - fraction[:, None], 0.0)
    above = jnp.where(columns == lower[:, None] + 1, fraction[:, None], 0.0)
    return (below + above).astype(jnp.float32)

def interpolate(coarse_block, rows_x, rows_y, rows_z):
    precise = lax.Precision.HIGHEST
    sectioned = jnp.einsum('abc,kc->abk', coarse_block, rows_z, precision=precise)
    sectioned = jnp.einsum('abk,jb->ajk', sectioned, rows_y, precision=precise)
    return jnp.einsum('ajk,ia->ijk', sectioned, rows_x, precision=precise)

def neighbours(values):
    return [values[2:, 1:-1, 1:-1], values[:-2, 1:-1, 1:-1], values[1:-1, 2:, 1:-1], values[1:-1, :-2, 1:-1], values[1:-1, 1:-1, 2:], values[1:-1, 1:-1, :-2]]

def balance(values, dielectric_pad, screening, charge):
    centre = values[1:-1, 1:-1, 1:-1]
    own_dielectric = dielectric_pad[1:-1, 1:-1, 1:-1]
    flux_sum = jnp.zeros_like(centre)
    weights = jnp.zeros_like(centre)
    for near_value, near_dielectric in zip(neighbours(values), neighbours(dielectric_pad)):
        coupling = 0.5 * (own_dielectric + near_dielectric)
        flux_sum = flux_sum + coupling * (centre - near_value)
        weights = weights + coupling
    residual = flux_sum + screening * jnp.sinh(centre) - charge
    return (residual, weights, centre)

def smooth(values, dielectric_pad, screening, charge, active):
    residual, weights, centre = balance(values, dielectric_pad, screening, charge)
    updated = jnp.where(active, centre - residual / (weights + screening * jnp.cosh(centre)), centre)
    return values.at[1:-1, 1:-1, 1:-1].set(updated)

def one_box(coarse, anchor, dielectric, screening, source):
    coarse_block = lax.dynamic_slice(coarse, (anchor[0], anchor[1], anchor[2]), (CBX, CBY, CBZ))
    potential = interpolate(coarse_block, spread(-1, FX + 2, CBX), spread(-1, FY + 2, CBY), spread(-1, FZ + 2, CBZ))
    dielectric_pad = jnp.pad(dielectric, 1)
    parity = (jnp.arange(FX, dtype=jnp.int32)[:, None, None] + jnp.arange(FY, dtype=jnp.int32)[None, :, None] + jnp.arange(FZ, dtype=jnp.int32)[None, None, :]) % 2
    for repeat in range(SWEEPS):
        for colour in (0, 1):
            potential = smooth(potential, dielectric_pad, screening, source, parity == colour)
    residual = balance(potential, dielectric_pad, screening, source)[0]
    box_norm = jnp.sqrt(jnp.mean(residual * residual) + 1e-06)
    return (potential[1:-1, 1:-1, 1:-1], box_norm)

def reference(coarse, anchors, dielectric, screening, source):
    potential, box_norm = lax.map(lambda packed: one_box(coarse, *packed), (anchors, dielectric, screening, source))
    return (potential, box_norm)
```

```python
import functools

import jax
import jax.numpy as jnp
from jax import lax
from jax.experimental import pallas as pl
from jax.experimental.pallas import tpu as pltpu
from jax.sharding import PartitionSpec as P

RATIO = 4
LOG2E = 1.4426950408889634
MESH = pl.DeviceIdType.MESH
F32 = jnp.float32


def iota(shape, dim):
    return lax.broadcasted_iota(jnp.int32, shape, dim)


def kernel(
    boxes, tx, ty, cells,
    anchors, coarse, diel, screen, source,
    pot_out, norm_out,
    slab, packed, arrived, zin, zfine, ylines, xlines,
    raw_e, raw_k, raw_s, eps, scr, chg, w, diag, u, pot,
    xsend, xrecv, ysend, yrecv, sums,
    slab_sem, raw_sem, pot_sem, pack_send, pack_recv,
    xs_sem, xr_sem, ys_sem, yr_sem, ss_sem, sr_sem,
):
    pairs = tx // 2
    nrows = (tx + 1) // RATIO + 2
    ncols = (ty + 1) // RATIO + 2
    slabs = slab.shape[1]
    deep = zin.shape[0] // ncols
    lines = ylines.shape[1] // (ty + 16)
    top = 8 + ty
    me = lax.axis_index("box")
    sx = lax.axis_index("sx")
    sy = lax.axis_index("sy")
    group = 2 * sx + sy
    peers = [{"sx": 1 - sx}, {"sy": 1 - sy}, {"sx": 1 - sx, "sy": 1 - sy}]

    barrier = pltpu.get_barrier_semaphore()

    def greet(d, _):
        pl.semaphore_signal(
            barrier, inc=1, device_id={"box": lax.rem(me + d, boxes)}, device_id_type=MESH
        )
        return 0

    lax.fori_loop(1, boxes, greet, 0)
    for peer in peers:
        pl.semaphore_signal(barrier, inc=1, device_id=peer, device_id_type=MESH)

    slab_in = [
        pltpu.make_async_copy(coarse.at[r], slab.at[:, r, :], slab_sem.at[r]) for r in range(slabs)
    ]
    raw_in = [
        pltpu.make_async_copy(src.at[0], dst, raw_sem.at[n])
        for n, (src, dst) in enumerate(((diel, raw_e), (screen, raw_k), (source, raw_s)))
    ]
    for copy in slab_in + raw_in:
        copy.start()
    for copy in slab_in:
        copy.wait()
    pl.semaphore_wait(barrier, boxes - 1 + 3)

    lane8 = iota((8, 128), 1)

    def window(d):
        b = lax.rem(me + d, boxes)
        y0 = anchors[b, 1] + sy * (ty // RATIO)
        z0 = anchors[b, 2]
        to_even = lax.rem(128 - z0, 128)
        to_odd = lax.rem(192 - z0, 128)
        parts = []
        extra = jnp.zeros((8, 128), F32)
        for m in range(ncols // 2):
            even = pltpu.roll(slab[y0 + 2 * m], to_even, 1)
            odd = pltpu.roll(slab[y0 + 2 * m + 1], to_odd, 1)
            parts.append(jnp.where(lane8 < 64, even, odd))
            ends = jnp.where(lane8 < 64, odd, even)
            if m > 0:
                ends = pltpu.roll(ends, 2 * m, 1)
            extra = jnp.where((lane8 % 64) // 2 == m, ends, extra)
        return parts + [extra]

    def send_window(d, _):
        for m, part in enumerate(window(d)):
            packed[d, m] = part
        pltpu.make_async_remote_copy(
            src_ref=packed.at[d],
            dst_ref=arrived.at[d],
            send_sem=pack_send,
            recv_sem=pack_recv,
            device_id={"box": lax.rem(me + d, boxes)},
            device_id_type=MESH,
        ).start()
        return 0

    lax.fori_loop(1, boxes, send_window, 0)
    for m, part in enumerate(window(0)):
        arrived[0, m] = part

    odd_tile = (iota((ty, 128), 0) + iota((ty, 128), 1)) % 2 == 1
    odd_tall = (iota((ty + 16, 128), 0) + iota((ty + 16, 128), 1)) % 2 == 1
    lane = iota((ty, 128), 1)

    def split(ref, k, h):
        low = ref[2 * k, :, pl.ds(128 * h, 128)]
        high = ref[2 * k + 1, :, pl.ds(128 * h, 128)]
        return jnp.where(odd_tile, high, low), jnp.where(odd_tile, low, high)

    def x_copy(slot):
        return pltpu.make_async_remote_copy(
            src_ref=xsend.at[slot], dst_ref=xrecv.at[slot],
            send_sem=xs_sem.at[slot], recv_sem=xr_sem.at[slot],
            device_id=peers[0], device_id_type=MESH,
        )

    def y_copy(slot):
        return pltpu.make_async_remote_copy(
            src_ref=ysend.at[slot], dst_ref=yrecv.at[slot],
            send_sem=ys_sem.at[slot], recv_sem=yr_sem.at[slot],
            device_id=peers[1], device_id_type=MESH,
        )

    x_edge = pairs - (pairs - 1) * sx
    x_halo = (pairs + 1) * (1 - sx)
    y_edge = top - 1 - (ty - 1) * sy
    y_halo = top - (ty + 1) * sy

    def send_halo(ref, colour, slot):
        for h in range(2):
            xsend[slot, h] = ref[colour, h, x_edge, 8:top, :]
        x_copy(slot).start()
        for h in range(2):
            for k in range(pairs):
                ysend[slot, h, k : k + 1, :] = ref[colour, h, k + 1, pl.ds(y_edge, 1), :]
        y_copy(slot).start()

    def take_halo(ref, colour, slot):
        x_copy(slot).wait_recv()
        for h in range(2):
            ref[colour, h, x_halo, 8:top, :] = xrecv[slot, h]
        y_copy(slot).wait_recv()
        for h in range(2):
            for k in range(pairs):
                ref[colour, h, k + 1, pl.ds(y_halo, 1), :] = yrecv[slot, h, k : k + 1, :]

    def around(ref, colour, kk):
        other = 1 - colour
        b = [ref[other, h, kk, 8:top, :] for h in range(2)]
        ends = ref[colour, 2, kk, 8:top, :]
        up = [pltpu.roll(v, 1, 1) for v in b]
        down = [pltpu.roll(v, 127, 1) for v in b]
        below = [jnp.where(lane == 0, ends, up[0]), jnp.where(lane == 0, up[0], up[1])]
        above = [jnp.where(lane == 127, down[1], down[0]), jnp.where(lane == 127, ends, down[1])]
        result = []
        for h in range(2):
            before = ref[other, h, kk - 1, 8:top, :]
            after = ref[other, h, kk + 1, 8:top, :]
            if colour == 0:
                outer = jnp.where(odd_tile, after, before)
            else:
                outer = jnp.where(odd_tile, before, after)
            result.append((
                b[h], outer,
                ref[other, h, kk, 7 : top - 1, :], ref[other, h, kk, 9 : top + 1, :],
                below[h], above[h],
            ))
        return result

    zero_tall = jnp.zeros((ty + 16, 128), F32)

    def clear(kk, _):
        for colour in range(2):
            for h in range(3):
                eps[colour, h, kk] = zero_tall
        return 0

    lax.fori_loop(0, pairs + 2, clear, 0)
    raw_in[0].wait()

    def split_eps(k, _):
        for h in range(2):
            red, black = split(raw_e, k, h)
            eps[0, h, k + 1, 8:top, :] = red
            eps[1, h, k + 1, 8:top, :] = black
        return 0

    lax.fori_loop(0, pairs, split_eps, 0)
    for colour in range(2):
        send_halo(eps, colour, colour)
    raw_in[1].wait()
    raw_in[2].wait()

    def split_rest(k, _):
        for h in range(2):
            for src, dst in ((raw_k, scr), (raw_s, chg)):
                red, black = split(src, k, h)
                dst[0, h, k] = red
                dst[1, h, k] = black
        return 0

    lax.fori_loop(0, pairs, split_rest, 0)
    for colour in range(2):
        take_halo(eps, colour, colour)

    def couple(k, _):
        for colour in range(2):
            near = around(eps, colour, k + 1)
            for h in range(2):
                own = eps[colour, h, k + 1, 8:top, :]
                total = None
                for n in range(6):
                    weight = 0.5 * (own + near[h][n])
                    w[colour, n, h, k] = weight
                    total = weight if total is None else total + weight
                diag[colour, h, k] = total
        return 0

    lax.fori_loop(0, pairs, couple, 0)

    row = iota((128, 128), 0)
    col = iota((128, 128), 1)
    pz = []
    for h in range(3):
        if h < 2:
            q = col + 128 * h + 1
        else:
            q = jnp.where(col == 0, 0, 257)
        low = q // RATIO
        part = (q - low * RATIO).astype(F32) / RATIO
        pz.append(
            (jnp.where(row == low, 1.0 - part, 0.0) + jnp.where(row == low + 1, part, 0.0)).astype(jnp.bfloat16)
        )

    pltpu.make_async_copy(arrived.at[pl.ds(1, boxes - 1)], arrived.at[pl.ds(1, boxes - 1)], pack_recv).wait()
    row0 = anchors[me, 0] + sx * (tx // RATIO)
    first = row0 // 8
    phase = row0 - first * 8
    for t in range(deep // 8):
        holder = jnp.minimum(first + t, boxes - 1)
        slot = lax.rem(me - holder + boxes, boxes)
        extra = arrived[slot, ncols // 2]
        for m in range(ncols // 2):
            part = arrived[slot, m]
            ends = pltpu.roll(extra, 128 - 2 * m, 1) if m > 0 else extra
            even = jnp.where(lane8 < 64, part, ends)
            odd = pltpu.roll(jnp.where(lane8 < 64, ends, part), 64, 1)
            zin[pl.ds((2 * m) * deep + 8 * t, 8), :] = even
            zin[pl.ds((2 * m + 1) * deep + 8 * t, 8), :] = odd
    values = zin[...]
    split_parts = []
    for _ in range(3):
        part = values.astype(jnp.bfloat16)
        split_parts.append(part)
        values = values - part.astype(F32)
    for h in range(3):
        zfine[h] = sum(jnp.dot(part, pz[h], preferred_element_type=F32) for part in reversed(split_parts))

    for h in range(3):
        columns = [zfine[h, pl.ds(c * deep + phase, lines), :] for c in range(ncols)]
        for q in range(ty + 2):
            low, part = q // RATIO, (q % RATIO) / RATIO
            value = columns[low]
            if part > 0:
                value = (1.0 - part) * value + part * columns[low + 1]
            ylines[h, pl.ds((q + 7) * lines, lines), :] = value
    for h in range(3):
        for r in range(nrows):
            xlines[h, r] = ylines[h, pl.ds(r, ty + 16, stride=lines), :]

    def guess(m, _):
        for h in range(3):
            before = xlines[h, jnp.maximum(m - 1, 0)]
            here = xlines[h, m]
            after = xlines[h, m + 1]
            planes = (
                (2 * m, 0.25 * before + 0.75 * here, here),
                (2 * m + 1, 0.75 * here + 0.25 * after, 0.5 * here + 0.5 * after),
            )
            for kk, low, high in planes:
                u[0, h, kk] = jnp.where(odd_tall, high, low)
                u[1, h, kk] = jnp.where(odd_tall, low, high)
        return 0

    lax.fori_loop(0, tx // RATIO + 1, guess, 0)

    def near_sum(colour, k):
        near = around(u, colour, k + 1)
        result = []
        for h in range(2):
            total = None
            for n in range(6):
                term = w[colour, n, h, k] * near[h][n]
                total = term if total is None else total + term
            result.append(total)
        return result

    def hyperbolic(value):
        power = value * LOG2E
        plus = jnp.exp2(power - 1.0)
        minus = jnp.exp2(-1.0 - power)
        return plus - minus, plus + minus

    def half_sweep(colour, last):
        def step(k, acc):
            pulls = near_sum(colour, k)
            for h in range(2):
                centre = u[colour, h, k + 1, 8:top, :]
                main = diag[colour, h, k]
                salt = scr[colour, h, k]
                pull = pulls[h] + chg[colour, h, k]
                sinh, cosh = hyperbolic(centre)
                g = main * centre - pull + salt * sinh
                d = main + salt * cosh
                value = centre - g / d
                u[colour, h, k + 1, 8:top, :] = value
                if last:
                    g = main * value - pull + salt * hyperbolic(value)[0]
                    acc = acc + g * g
            return acc

        if last:
            return lax.fori_loop(0, pairs, step, jnp.zeros((ty, 128), F32))
        lax.fori_loop(0, pairs, lambda k, c: step(k, c), 0)
        return None

    for turn in range(4):
        colour = turn % 2
        total = half_sweep(colour, turn == 3)
        send_halo(u, colour, 2 + turn)
        if turn < 3:
            take_halo(u, colour, 2 + turn)

    def join(k, _):
        for h in range(2):
            red = u[0, h, k + 1, 8:top, :]
            black = u[1, h, k + 1, 8:top, :]
            pot[2 * k, :, pl.ds(128 * h, 128)] = jnp.where(odd_tile, black, red)
            pot[2 * k + 1, :, pl.ds(128 * h, 128)] = jnp.where(odd_tile, red, black)
        return 0

    lax.fori_loop(0, pairs, join, 0)
    pot_copy = pltpu.make_async_copy(pot, pot_out.at[0], pot_sem)
    pot_copy.start()
    take_halo(u, 1, 5)

    def remainder(k, acc):
        pulls = near_sum(0, k)
        for h in range(2):
            centre = u[0, h, k + 1, 8:top, :]
            pull = pulls[h] + chg[0, h, k]
            g = diag[0, h, k] * centre - pull + scr[0, h, k] * hyperbolic(centre)[0]
            acc = acc + g * g
        return acc

    total = lax.fori_loop(0, pairs, remainder, total)
    part = total[0:8]
    for t in range(1, ty // 8):
        part = part + total[8 * t : 8 * t + 8]
    sums[group] = part
    sum_copies = [
        pltpu.make_async_remote_copy(
            src_ref=sums.at[group], dst_ref=sums.at[group],
            send_sem=ss_sem.at[n], recv_sem=sr_sem.at[n],
            device_id=peer, device_id_type=MESH,
        )
        for n, peer in enumerate(peers)
    ]
    for copy in sum_copies:
        copy.start()

    pltpu.make_async_copy(packed.at[pl.ds(1, boxes - 1)], packed.at[pl.ds(1, boxes - 1)], pack_send).wait()
    for slot in range(6):
        x_copy(slot).wait_send()
        y_copy(slot).wait_send()
    for copy in sum_copies:
        copy.wait()
    squares = jnp.sum(sums[0] + sums[1] + sums[2] + sums[3], keepdims=True)
    norm_out[...] = jnp.sqrt(squares / cells + 1e-06)
    pot_copy.wait()


def body(coarse, anchors, dielectric, screening, source):
    boxes = lax.axis_size("box")
    _, tx, ty, tz = dielectric.shape
    pairs = tx // 2
    nrows = (tx + 1) // RATIO + 2
    ncols = (ty + 1) // RATIO + 2
    deep = (nrows + 14) // 8 * 8
    lines = (nrows + 7) // 8 * 8
    slabs, gy, gz = coarse.shape
    cells = tx * ty * tz * lax.axis_size("sx") * lax.axis_size("sy")
    any_spec = pl.BlockSpec(memory_space=pl.ANY)
    dma = pltpu.SemaphoreType.DMA

    def vmem(*shape):
        return pltpu.VMEM(shape, F32)

    potential, norm = pl.pallas_call(
        functools.partial(kernel, boxes, tx, ty, cells),
        out_shape=(
            jax.ShapeDtypeStruct((1, tx, ty, tz), F32),
            jax.ShapeDtypeStruct((1, 1), F32),
        ),
        in_specs=[pl.BlockSpec(memory_space=pltpu.SMEM)] + [any_spec] * 4,
        out_specs=(any_spec, pl.BlockSpec(memory_space=pltpu.VMEM)),
        scratch_shapes=[
            vmem(gy, slabs, gz),
            vmem(boxes, ncols // 2 + 1, 8, 128),
            vmem(boxes, ncols // 2 + 1, 8, 128),
            vmem(ncols * deep, 128),
            vmem(3, ncols * deep, 128),
            vmem(3, (ty + 16) * lines, 128),
            vmem(3, nrows, ty + 16, 128),
            vmem(tx, ty, tz),
            vmem(tx, ty, tz),
            vmem(tx, ty, tz),
            vmem(2, 3, pairs + 2, ty + 16, 128),
            vmem(2, 2, pairs, ty, 128),
            vmem(2, 2, pairs, ty, 128),
            vmem(2, 6, 2, pairs, ty, 128),
            vmem(2, 2, pairs, ty, 128),
            vmem(2, 3, pairs + 2, ty + 16, 128),
            vmem(tx, ty, tz),
            vmem(6, 2, ty, 128),
            vmem(6, 2, ty, 128),
            vmem(6, 2, pairs, 128),
            vmem(6, 2, pairs, 128),
            vmem(4, 8, 128),
            dma((slabs,)), dma((3,)), dma, dma, dma,
            dma((6,)), dma((6,)), dma((6,)), dma((6,)), dma((3,)), dma((3,)),
        ],
        compiler_params=pltpu.CompilerParams(
            collective_id=0, has_side_effects=True, vmem_limit_bytes=56 * 1024 * 1024
        ),
        cost_estimate=pl.CostEstimate(
            flops=200 * tx * ty * tz, bytes_accessed=16 * tx * ty * tz, transcendentals=12 * tx * ty * tz
        ),
    )(anchors, coarse, dielectric, screening, source)
    return potential, norm.reshape(1)


def solution(mesh):
    tile = P("box", "sx", "sy", None)
    return jax.shard_map(
        body,
        mesh=mesh,
        in_specs=(P("box", None, None), P(), tile, tile, tile),
        out_specs=(tile, P("box")),
        check_vma=False,
    )
```

```python
import functools

import jax
import jax.numpy as jnp
from jax import lax
from jax.experimental import pallas as pl
from jax.experimental.pallas import tpu as pltpu
from jax.sharding import PartitionSpec as P

RATIO = 4
LOG2E = 1.4426950408889634
MESH = pl.DeviceIdType.MESH
F32 = jnp.float32


def iota(shape, dim):
    return lax.broadcasted_iota(jnp.int32, shape, dim)


def loop(count, step, carry, unroll):
    chunks = count // unroll if count > unroll else 0

    def chunk(n, carry):
        for i in range(unroll):
            carry = step(n * unroll + i, carry)
        return carry

    if chunks:
        carry = lax.fori_loop(0, chunks, chunk, carry)
    for i in range(chunks * unroll, count):
        carry = step(i, carry)
    return carry


def kernel(
    boxes, tx, ty, cells,
    anchors_in, coarse, diel, screen, source,
    pot, norm_out,
    anchors, slab, packed, arrived, zin, zfine, ylines, xlines,
    raw_e, raw_k, raw_s, er, eb, scr, chg, w, diag, ur, ub, uend,
    wx, dx, wy, dy, line_r, line_b, line_end,
    sxs, sxr, sys, syr, sds, sdr, dxs, dxr, dys, dyr, dds, ddr, sums,
    anchor_sem, slab_sem, raw_sem, pack_send, pack_recv, halo_send, halo_recv, ss_sem, sr_sem,
):
    pairs = tx // 2
    nrows = (tx + 1) // RATIO + 2
    ncols = (ty + 1) // RATIO + 2
    slabs = slab.shape[1]
    deep = zin.shape[0] // ncols
    lines = ylines.shape[1] // (ty + 16)
    top = 8 + ty
    me = lax.axis_index("box")
    sx = lax.axis_index("sx")
    sy = lax.axis_index("sy")
    group = 2 * sx + sy
    peers = [{"sx": 1 - sx}, {"sy": 1 - sy}, {"sx": 1 - sx, "sy": 1 - sy}]

    x_edge = pairs - (pairs - 1) * sx
    x_halo = (pairs + 1) * (1 - sx)
    x_far = (pairs + 1) * sx
    y_edge = top - 1 - (ty - 1) * sy
    y_next = y_edge - 1 + 2 * sy
    y_halo = top - (ty + 1) * sy

    anchor_in = pltpu.make_async_copy(anchors_in, anchors, anchor_sem)
    slab_in = [
        pltpu.make_async_copy(coarse.at[r], slab.at[:, r, :], slab_sem.at[r]) for r in range(slabs)
    ]
    raw_in = [
        pltpu.make_async_copy(src.at[0], dst, raw_sem.at[n])
        for n, (src, dst) in enumerate(((diel, raw_e), (screen, raw_k), (source, raw_s)))
    ]
    anchor_in.start()
    for copy in slab_in:
        copy.start()

    barrier = pltpu.get_barrier_semaphore()

    def greet(d, _):
        pl.semaphore_signal(
            barrier, inc=1, device_id={"box": lax.rem(me + d, boxes)}, device_id_type=MESH
        )
        return 0

    lax.fori_loop(1, boxes, greet, 0)
    for peer in peers:
        pl.semaphore_signal(barrier, inc=1, device_id=peer, device_id_type=MESH)
    for copy in raw_in:
        copy.start()

    lane8 = iota((8, 128), 1)

    def window(d):
        b = lax.rem(me + d, boxes)
        y0 = anchors[1, b] + sy * (ty // RATIO)
        z0 = anchors[2, b]
        to_even = lax.rem(128 - z0, 128)
        to_odd = lax.rem(192 - z0, 128)
        parts = []
        extra = jnp.zeros((8, 128), F32)
        for m in range(ncols // 2):
            even = pltpu.roll(slab[y0 + 2 * m], to_even, 1)
            odd = pltpu.roll(slab[y0 + 2 * m + 1], to_odd, 1)
            parts.append(jnp.where(lane8 < 64, even, odd))
            ends = jnp.where(lane8 < 64, odd, even)
            if m > 0:
                ends = pltpu.roll(ends, 2 * m, 1)
            extra = jnp.where((lane8 % 64) // 2 == m, ends, extra)
        return parts + [extra]

    def pack_window(d, _):
        for m, part in enumerate(window(d + 1)):
            packed[d + 1, m] = part
        return 0

    def send_window(d, _):
        pltpu.make_async_remote_copy(
            src_ref=packed.at[d],
            dst_ref=arrived.at[d],
            send_sem=pack_send,
            recv_sem=pack_recv,
            device_id={"box": lax.rem(me + d, boxes)},
            device_id_type=MESH,
        ).start()
        return 0

    anchor_in.wait()
    for copy in slab_in:
        copy.wait()
    loop(boxes - 1, pack_window, 0, 4)
    pl.semaphore_wait(barrier, boxes - 1 + 3)
    lax.fori_loop(1, boxes, send_window, 0)
    for m, part in enumerate(window(0)):
        arrived[0, m] = part

    odd_tile = (iota((ty, 128), 0) + iota((ty, 128), 1)) % 2 == 1
    odd_tall = (iota((ty + 16, 128), 0) + iota((ty + 16, 128), 1)) % 2 == 1
    odd8 = (iota((8, 128), 0) + iota((8, 128), 1)) % 2 == 1
    odd_line = (iota((pairs, 128), 1) + y_halo) % 2 == 1

    halo_src = [[sxs, sys, sds]] + [[dxs.at[t], dys.at[t], dds.at[t]] for t in range(2)]
    halo_dst = [[sxr, syr, sdr]] + [[dxr.at[t], dyr.at[t], ddr.at[t]] for t in range(2)]

    def halo_copies(slot):
        return [
            pltpu.make_async_remote_copy(
                src_ref=halo_src[slot][n], dst_ref=halo_dst[slot][n],
                send_sem=halo_send.at[3 * slot + n], recv_sem=halo_recv.at[3 * slot + n],
                device_id=peers[n], device_id_type=MESH,
            )
            for n in range(3)
        ]

    def around(ref, ends, colour, kk, r0, rows, odd, outer=None):
        lane = iota((rows, 128), 1)
        here = pl.ds(r0 + 8, rows)
        b = [ref[h, kk, here, :] for h in range(2)]
        below, above = along_z(b, ends, lane)
        result = []
        for h in range(2):
            if outer is None:
                before = ref[h, kk - 1, here, :]
                after = ref[h, kk + 1, here, :]
                side = jnp.where(odd, after, before) if colour == 0 else jnp.where(odd, before, after)
            else:
                side = ref[h, outer, here, :]
            result.append([
                b[h], side, ref[h, kk, pl.ds(r0 + 7, rows), :], ref[h, kk, pl.ds(r0 + 9, rows), :],
                below[h], above[h],
            ])
        return result

    def along_z(b, ends, lane):
        up = [pltpu.roll(v, 1, 1) for v in b]
        down = [pltpu.roll(v, 127, 1) for v in b]
        below = [jnp.where(lane == 0, ends, up[0]), jnp.where(lane == 0, up[0], up[1])]
        above = [jnp.where(lane == 127, down[1], down[0]), jnp.where(lane == 127, ends, down[1])]
        return below, above

    def around_line(own_edge, far, ends):
        b = [line_r[h, pl.ds(1, pairs), :] for h in range(2)]
        below, above = along_z(b, ends, iota((pairs, 128), 1))
        result = []
        for h in range(2):
            before = line_r[h, pl.ds(0, pairs), :]
            after = line_r[h, pl.ds(2, pairs), :]
            side = jnp.where(odd_line, before, after)
            result.append([b[h], side, own_edge[h], far[h], below[h], above[h]])
        return result

    def rows_to(dst, ref, row, first):
        for h in range(2):
            for k in range(pairs):
                dst[h, k : k + 1, :] = ref[h, k + first, pl.ds(row, 1), :]

    def rows_from(src, ref):
        for h in range(2):
            for k in range(pairs):
                ref[h, k + 1, pl.ds(y_halo, 1), :] = src[h, k : k + 1, :]

    def corner_to(dst, ref):
        for h in range(2):
            dst[h : h + 1, :] = ref[h, x_edge, pl.ds(y_edge, 1), :]

    def take_red(ref, xr, yr, dr, outside):
        for h in range(2):
            ref[h, x_halo, 8:top, :] = xr[h]
            ref[h, x_halo, pl.ds(y_halo, 1), :] = dr[h : h + 1, :]
            line_r[h, pl.ds(1, pairs), :] = yr[h]
            line_r[h, pl.ds(x_halo, 1), :] = dr[h : h + 1, :]
            line_r[h, pl.ds(x_far, 1), :] = outside[h]
        rows_from(yr, ref)

    zero_tall = jnp.zeros((ty + 16, 128), F32)

    def clear(kk, _):
        for h in range(2):
            er[h, kk] = zero_tall
            eb[h, kk] = zero_tall
        return 0

    lax.fori_loop(0, pairs + 2, clear, 0)
    sds[...] = jnp.zeros((8, 128), F32)
    for t in range(2):
        dds[t] = jnp.zeros((8, 128), F32)

    def split(ref, k, h):
        low = ref[2 * k, :, pl.ds(128 * h, 128)]
        high = ref[2 * k + 1, :, pl.ds(128 * h, 128)]
        return jnp.where(odd_tile, high, low), jnp.where(odd_tile, low, high)

    def split_eps(k, _):
        for h in range(2):
            er[h, k + 1, 8:top, :], eb[h, k + 1, 8:top, :] = split(raw_e, k, h)
        return 0

    def split_rest(k, _):
        for h in range(2):
            for src, dst in ((raw_k, scr), (raw_s, chg)):
                dst[0, h, k], dst[1, h, k] = split(src, k, h)
        return 0

    raw_in[0].wait()
    loop(pairs, split_eps, 0, 2)
    raw_in[1].wait()
    raw_in[2].wait()
    loop(pairs, split_rest, 0, 2)
    for h in range(2):
        sxs[0, h] = er[h, x_edge, 8:top, :]
        sxs[1, h] = eb[h, x_edge, 8:top, :]
        sxs[2, h] = scr[1, h, x_edge - 1]
        sxs[3, h] = chg[1, h, x_edge - 1]
    rows_to(sys.at[0], er, y_edge, 1)
    rows_to(sys.at[1], er, y_next, 1)
    rows_to(sys.at[2], eb, y_edge, 1)
    rows_to(sys.at[3], scr.at[1], y_edge - 8, 0)
    rows_to(sys.at[4], chg.at[1], y_edge - 8, 0)
    corner_to(sds, er)
    for copy in halo_copies(0):
        copy.start()
    for copy in halo_copies(0):
        copy.wait_recv()
    zero_line = jnp.zeros((1, 128), F32)
    take_red(er, sxr.at[0], syr.at[0], sdr, (zero_line, zero_line))
    for h in range(2):
        eb[h, x_halo, 8:top, :] = sxr[1, h]
    rows_from(syr.at[2], eb)

    def weigh(own, near):
        weights = [0.5 * (own + value) for value in near]
        return weights, sum(weights[1:], weights[0])

    def couple(k, _):
        for colour, mine, other in ((0, er, eb), (1, eb, er)):
            near = around(other, 0.0, colour, k + 1, 0, ty, odd_tile)
            for h in range(2):
                weights, total = weigh(mine[h, k + 1, 8:top, :], near[h])
                for n in range(6):
                    w[colour, n, h, k] = weights[n]
                diag[colour, h, k] = total
        return 0

    loop(pairs, couple, 0, 2)
    near_x = around(er, 0.0, 1, x_halo, 0, ty, odd_tile, x_edge)
    near_y = around_line(sys[0], syr[1], 0.0)
    for h in range(2):
        weights, dx[h] = weigh(eb[h, x_halo, 8:top, :], near_x[h])
        for n in range(6):
            wx[n, h] = weights[n]
        weights, dy[h] = weigh(syr[2, h], near_y[h])
        for n in range(6):
            wy[n, h] = weights[n]

    row = iota((128, 128), 0)
    col = iota((128, 128), 1)
    pz = []
    for h in range(3):
        if h < 2:
            q = col + 128 * h + 1
        else:
            q = jnp.where(col == 0, 0, 257)
        low = q // RATIO
        part = (q - low * RATIO).astype(F32) / RATIO
        pz.append(
            (jnp.where(row == low, 1.0 - part, 0.0) + jnp.where(row == low + 1, part, 0.0)).astype(jnp.bfloat16)
        )

    pltpu.make_async_copy(arrived.at[pl.ds(1, boxes - 1)], arrived.at[pl.ds(1, boxes - 1)], pack_recv).wait()
    row0 = anchors[0, me] + sx * (tx // RATIO)
    first = row0 // 8
    phase = row0 - first * 8
    for t in range(deep // 8):
        holder = jnp.minimum(first + t, boxes - 1)
        slot = lax.rem(me - holder + boxes, boxes)
        extra = arrived[slot, ncols // 2]
        for m in range(ncols // 2):
            part = arrived[slot, m]
            ends = pltpu.roll(extra, 128 - 2 * m, 1) if m > 0 else extra
            even = jnp.where(lane8 < 64, part, ends)
            odd = pltpu.roll(jnp.where(lane8 < 64, ends, part), 64, 1)
            zin[pl.ds((2 * m) * deep + 8 * t, 8), :] = even
            zin[pl.ds((2 * m + 1) * deep + 8 * t, 8), :] = odd
    values = zin[...]
    split_parts = []
    for _ in range(3):
        part = values.astype(jnp.bfloat16)
        split_parts.append(part)
        values = values - part.astype(F32)
    for h in range(3):
        zfine[h] = sum(jnp.dot(part, pz[h], preferred_element_type=F32) for part in reversed(split_parts))

    for h in range(3):
        columns = [zfine[h, pl.ds(c * deep + phase, lines), :] for c in range(ncols)]
        for q in range(ty + 2):
            low, part = q // RATIO, (q % RATIO) / RATIO
            value = columns[low]
            if part > 0:
                value = (1.0 - part) * value + part * columns[low + 1]
            ylines[h, pl.ds((q + 7) * lines, lines), :] = value
    for h in range(3):
        for r in range(nrows):
            xlines[h, r] = ylines[h, pl.ds(r, ty + 16, stride=lines), :]

    def guess(m, _):
        for h in range(3):
            before = xlines[h, jnp.maximum(m - 1, 0)]
            here = xlines[h, m]
            after = xlines[h, m + 1]
            planes = (
                (2 * m, 0.25 * before + 0.75 * here, here),
                (2 * m + 1, 0.75 * here + 0.25 * after, 0.5 * here + 0.5 * after),
            )
            for kk, low, high in planes:
                red = jnp.where(odd_tall, high, low)
                black = jnp.where(odd_tall, low, high)
                if h < 2:
                    ur[h, kk] = red
                    ub[h, kk] = black
                else:
                    uend[0, kk] = red
                    uend[1, kk] = black
        return 0

    loop(tx // RATIO + 1, guess, 0, 2)

    def hyperbolic(value):
        power = value * LOG2E
        plus = jnp.exp2(power - 1.0)
        minus = jnp.exp2(-1.0 - power)
        return plus - minus, plus + minus

    def weighted(weights, near):
        total = weights(0) * near[0]
        for n in (4, 5, 1, 2, 3):
            total = total + weights(n) * near[n]
        return total

    def newton(centre, pull, main, salt):
        sinh, cosh = hyperbolic(centre)
        return centre - (main * centre - pull + salt * sinh) / (main + salt * cosh)

    def square(centre, pull, main, salt):
        g = main * centre - pull + salt * hyperbolic(centre)[0]
        return g * g

    def cells_of(colour, kk, r0, acc, update, residual):
        here = pl.ds(r0, 8)
        own, other = (ur, ub) if colour == 0 else (ub, ur)
        k = kk - 1
        near = around(other, uend[colour, kk, pl.ds(r0 + 8, 8), :], colour, kk, r0, 8, odd8)
        for h in range(2):
            pull = weighted(lambda n: w[colour, n, h, k, here, :], near[h]) + chg[colour, h, k, here, :]
            main = diag[colour, h, k, here, :]
            salt = scr[colour, h, k, here, :]
            value = own[h, kk, pl.ds(r0 + 8, 8), :]
            if update:
                value = newton(value, pull, main, salt)
                own[h, kk, pl.ds(r0 + 8, 8), :] = value
            if residual:
                acc = acc + square(value, pull, main, salt)
        return acc

    inner_pair = 1 + sx
    inner_row = pl.multiple_of(8 * sy, 8)
    edge_row = pl.multiple_of((ty - 8) * (1 - sy), 8)

    def edge(colour, acc, residual):
        for r0 in range(0, ty, 8):
            acc = cells_of(colour, x_edge, r0, acc, True, residual)
        return loop(
            pairs - 1,
            lambda i, acc: cells_of(colour, inner_pair + i, edge_row, acc, True, residual),
            acc, pairs,
        )

    def interior(colour, acc, residual):
        def step(i, acc):
            for s in range(ty // 8 - 1):
                acc = cells_of(colour, inner_pair + i, pl.multiple_of(inner_row + 8 * s, 8), acc, True, residual)
            return acc

        return loop(pairs - 1, step, acc, 5)

    def send_red(t):
        for h in range(2):
            dxs[t, h] = ur[h, x_edge, 8:top, :]
        rows_to(dys.at[t, 0], ur, y_edge, 1)
        rows_to(dys.at[t, 1], ur, y_next, 1)
        corner_to(dds.at[t], ur)
        for copy in halo_copies(1 + t):
            copy.start()

    def take(t):
        for copy in halo_copies(1 + t):
            copy.wait_recv()
        outside = [ur[h, x_far, pl.ds(y_halo, 1), :] for h in range(2)]
        take_red(ur, dxr.at[t], dyr.at[t, 0], ddr.at[t], outside)

    def beside(t):
        near_x = around(ur, uend[1, x_halo, 8:top, :], 1, x_halo, 0, ty, odd_tile, x_edge)
        near_y = around_line(dys[t, 0], dyr[t, 1], line_end[...])
        for h in range(2):
            pull = weighted(lambda n: wx[n, h], near_x[h]) + sxr[3, h]
            ub[h, x_halo, 8:top, :] = newton(ub[h, x_halo, 8:top, :], pull, dx[h], sxr[2, h])
            pull = weighted(lambda n: wy[n, h], near_y[h]) + syr[4, h]
            line_b[h] = newton(line_b[h], pull, dy[h], syr[3, h])
        rows_from(line_b, ub)

    rows_to(line_b, ub, y_halo, 1)
    for k in range(pairs):
        line_end[k : k + 1, :] = uend[1, k + 1, pl.ds(y_halo, 1), :]
    total = jnp.zeros((8, 128), F32)
    for t in range(2):
        edge(0, total, False)
        send_red(t)
        interior(0, total, False)
        total = interior(1, total, t == 1)
        take(t)
        beside(t)
        total = edge(1, total, t == 1)

    def remainder(i, acc):
        for r0 in range(0, ty, 8):
            acc = cells_of(0, i + 1, r0, acc, False, True)
        return acc

    sums[group] = loop(pairs, remainder, total, 5)
    sum_copies = [
        pltpu.make_async_remote_copy(
            src_ref=sums.at[group], dst_ref=sums.at[group],
            send_sem=ss_sem.at[n], recv_sem=sr_sem.at[n],
            device_id=peer, device_id_type=MESH,
        )
        for n, peer in enumerate(peers)
    ]
    for copy in sum_copies:
        copy.start()

    def join(k, _):
        for h in range(2):
            red = ur[h, k + 1, 8:top, :]
            black = ub[h, k + 1, 8:top, :]
            pot[0, 2 * k, :, pl.ds(128 * h, 128)] = jnp.where(odd_tile, black, red)
            pot[0, 2 * k + 1, :, pl.ds(128 * h, 128)] = jnp.where(odd_tile, red, black)
        return 0

    loop(pairs, join, 0, 2)

    pltpu.make_async_copy(packed.at[pl.ds(1, boxes - 1)], packed.at[pl.ds(1, boxes - 1)], pack_send).wait()
    for slot in range(3):
        for copy in halo_copies(slot):
            copy.wait_send()
    for copy in sum_copies:
        copy.wait()
    squares = jnp.sum(sums[0] + sums[1] + sums[2] + sums[3], keepdims=True)
    norm_out[...] = jnp.sqrt(squares / cells + 1e-06)


def body(coarse, anchors, dielectric, screening, source):
    boxes = lax.axis_size("box")
    _, tx, ty, tz = dielectric.shape
    pairs = tx // 2
    nrows = (tx + 1) // RATIO + 2
    ncols = (ty + 1) // RATIO + 2
    deep = (nrows + 14) // 8 * 8
    lines = (nrows + 7) // 8 * 8
    slabs, gy, gz = coarse.shape
    cells = tx * ty * tz * lax.axis_size("sx") * lax.axis_size("sy")
    any_spec = pl.BlockSpec(memory_space=pl.ANY)
    vmem_spec = pl.BlockSpec(memory_space=pltpu.VMEM)
    dma = pltpu.SemaphoreType.DMA

    def vmem(*shape):
        return pltpu.VMEM(shape, F32)

    def padded():
        return vmem(2, pairs + 2, ty + 16, 128)

    potential, norm = pl.pallas_call(
        functools.partial(kernel, boxes, tx, ty, cells),
        out_shape=(
            jax.ShapeDtypeStruct((1, tx, ty, tz), F32),
            jax.ShapeDtypeStruct((1, 1), F32),
        ),
        in_specs=[any_spec] * 5,
        out_specs=(vmem_spec, vmem_spec),
        scratch_shapes=[
            pltpu.SMEM((3, boxes), jnp.int32),
            vmem(gy, slabs, gz),
            vmem(boxes, ncols // 2 + 1, 8, 128),
            vmem(boxes, ncols // 2 + 1, 8, 128),
            vmem(ncols * deep, 128),
            vmem(3, ncols * deep, 128),
            vmem(3, (ty + 16) * lines, 128),
            vmem(3, nrows, ty + 16, 128),
            vmem(tx, ty, tz),
            vmem(tx, ty, tz),
            vmem(tx, ty, tz),
            padded(),
            padded(),
            vmem(2, 2, pairs, ty, 128),
            vmem(2, 2, pairs, ty, 128),
            vmem(2, 6, 2, pairs, ty, 128),
            vmem(2, 2, pairs, ty, 128),
            padded(),
            padded(),
            padded(),
            vmem(6, 2, ty, 128),
            vmem(2, ty, 128),
            vmem(6, 2, pairs, 128),
            vmem(2, pairs, 128),
            vmem(2, pairs + 4, 128),
            vmem(2, pairs, 128),
            vmem(pairs, 128),
            vmem(4, 2, ty, 128),
            vmem(4, 2, ty, 128),
            vmem(5, 2, pairs, 128),
            vmem(5, 2, pairs, 128),
            vmem(8, 128),
            vmem(8, 128),
            vmem(2, 2, ty, 128),
            vmem(2, 2, ty, 128),
            vmem(2, 2, 2, pairs, 128),
            vmem(2, 2, 2, pairs, 128),
            vmem(2, 8, 128),
            vmem(2, 8, 128),
            vmem(4, 8, 128),
            dma, dma((slabs,)), dma((3,)), dma, dma, dma((9,)), dma((9,)), dma((3,)), dma((3,)),
        ],
        compiler_params=pltpu.CompilerParams(
            collective_id=0, has_side_effects=True, vmem_limit_bytes=52 * 1024 * 1024
        ),
        cost_estimate=pl.CostEstimate(
            flops=200 * tx * ty * tz, bytes_accessed=16 * tx * ty * tz, transcendentals=12 * tx * ty * tz
        ),
    )(anchors.T, coarse, dielectric, screening, source)
    return potential, norm.reshape(1)


def solution(mesh):
    tile = P("box", "sx", "sy", None)
    return jax.shard_map(
        body,
        mesh=mesh,
        in_specs=(P("box", None, None), P(), tile, tile, tile),
        out_specs=(tile, P("box")),
        check_vma=False,
    )
```

```python
import functools

import jax
import jax.numpy as jnp
from jax import lax
from jax.experimental import pallas as pl
from jax.experimental.pallas import tpu as pltpu
from jax.sharding import PartitionSpec as P

RATIO = 4
LOG2E = 1.4426950408889634
MESH = pl.DeviceIdType.MESH
F32 = jnp.float32


def iota(shape, dim):
    return lax.broadcasted_iota(jnp.int32, shape, dim)


def loop(count, step, carry, unroll):
    chunks = count // unroll if count > unroll else 0

    def chunk(n, carry):
        for i in range(unroll):
            carry = step(n * unroll + i, carry)
        return carry

    if chunks:
        carry = lax.fori_loop(0, chunks, chunk, carry)
    for i in range(chunks * unroll, count):
        carry = step(i, carry)
    return carry


def kernel(
    boxes, tx, ty, cells,
    anchors_in, coarse, diel, screen, source,
    pot, norm_out,
    anchors, slab, packed, arrived, zin, zfine, ylines, xlines,
    raw_e, raw_k, raw_s, er, eb, scr, chg, w, diag, ur, ub, uend,
    wx, dx, wy, dy, line_r, line_b, line_end,
    sxs, sxr, sys, syr, sds, sdr, dxs, dxr, dys, dyr, dds, ddr, sums,
    anchor_sem, slab_sem, raw_sem, pack_send, pack_recv, halo_send, halo_recv, ss_sem, sr_sem,
):
    pairs = tx // 2
    nrows = (tx + 1) // RATIO + 2
    ncols = (ty + 1) // RATIO + 2
    slabs = slab.shape[1]
    deep = zin.shape[0] // ncols
    lines = ylines.shape[1] // (ty + 16)
    top = 8 + ty
    me = lax.axis_index("box")
    sx = lax.axis_index("sx")
    sy = lax.axis_index("sy")
    group = 2 * sx + sy
    peers = [{"sx": 1 - sx}, {"sy": 1 - sy}, {"sx": 1 - sx, "sy": 1 - sy}]

    x_edge = pairs - (pairs - 1) * sx
    x_halo = (pairs + 1) * (1 - sx)
    x_far = (pairs + 1) * sx
    y_edge = top - 1 - (ty - 1) * sy
    y_next = y_edge - 1 + 2 * sy
    y_halo = top - (ty + 1) * sy

    anchor_in = pltpu.make_async_copy(anchors_in, anchors, anchor_sem)
    slab_in = [
        pltpu.make_async_copy(coarse.at[r], slab.at[:, r, :], slab_sem.at[r]) for r in range(slabs)
    ]
    raw_in = [
        pltpu.make_async_copy(src.at[0], dst, raw_sem.at[n])
        for n, (src, dst) in enumerate(((diel, raw_e), (screen, raw_k), (source, raw_s)))
    ]
    anchor_in.start()
    for copy in slab_in:
        copy.start()

    barrier = pltpu.get_barrier_semaphore()

    def greet(d, _):
        pl.semaphore_signal(
            barrier, inc=1, device_id={"box": lax.rem(me + d, boxes)}, device_id_type=MESH
        )
        return 0

    lax.fori_loop(1, boxes, greet, 0)
    for peer in peers:
        pl.semaphore_signal(barrier, inc=1, device_id=peer, device_id_type=MESH)
    for copy in raw_in:
        copy.start()

    lane8 = iota((8, 128), 1)

    def window(d):
        b = lax.rem(me + d, boxes)
        y0 = anchors[1, b] + sy * (ty // RATIO)
        z0 = anchors[2, b]
        to_even = lax.rem(128 - z0, 128)
        to_odd = lax.rem(192 - z0, 128)
        parts = []
        extra = jnp.zeros((8, 128), F32)
        for m in range(ncols // 2):
            even = pltpu.roll(slab[y0 + 2 * m], to_even, 1)
            odd = pltpu.roll(slab[y0 + 2 * m + 1], to_odd, 1)
            parts.append(jnp.where(lane8 < 64, even, odd))
            ends = jnp.where(lane8 < 64, odd, even)
            if m > 0:
                ends = pltpu.roll(ends, 2 * m, 1)
            extra = jnp.where((lane8 % 64) // 2 == m, ends, extra)
        return parts + [extra]

    def pack_window(d, _):
        for m, part in enumerate(window(d + 1)):
            packed[d + 1, m] = part
        return 0

    def send_window(d, _):
        pltpu.make_async_remote_copy(
            src_ref=packed.at[d],
            dst_ref=arrived.at[d],
            send_sem=pack_send,
            recv_sem=pack_recv,
            device_id={"box": lax.rem(me + d, boxes)},
            device_id_type=MESH,
        ).start()
        return 0

    anchor_in.wait()
    for copy in slab_in:
        copy.wait()
    loop(boxes - 1, pack_window, 0, 4)
    pl.semaphore_wait(barrier, boxes - 1 + 3)
    lax.fori_loop(1, boxes, send_window, 0)
    for m, part in enumerate(window(0)):
        arrived[0, m] = part

    odd_tile = (iota((ty, 128), 0) + iota((ty, 128), 1)) % 2 == 1
    odd_tall = (iota((ty + 16, 128), 0) + iota((ty + 16, 128), 1)) % 2 == 1
    odd8 = (iota((8, 128), 0) + iota((8, 128), 1)) % 2 == 1
    odd_line = (iota((pairs, 128), 1) + y_halo) % 2 == 1

    halo_src = [[sxs, sys, sds]] + [[dxs.at[t], dys.at[t], dds.at[t]] for t in range(2)]
    halo_dst = [[sxr, syr, sdr]] + [[dxr.at[t], dyr.at[t], ddr.at[t]] for t in range(2)]

    def halo_copies(slot):
        return [
            pltpu.make_async_remote_copy(
                src_ref=halo_src[slot][n], dst_ref=halo_dst[slot][n],
                send_sem=halo_send.at[3 * slot + n], recv_sem=halo_recv.at[3 * slot + n],
                device_id=peers[n], device_id_type=MESH,
            )
            for n in range(3)
        ]

    def around(ref, ends, colour, kk, r0, rows, odd, outer=None):
        lane = iota((rows, 128), 1)
        here = pl.ds(r0 + 8, rows)
        b = [ref[h, kk, here, :] for h in range(2)]
        below, above = along_z(b, ends, lane)
        result = []
        for h in range(2):
            if outer is None:
                before = ref[h, kk - 1, here, :]
                after = ref[h, kk + 1, here, :]
                side = jnp.where(odd, after, before) if colour == 0 else jnp.where(odd, before, after)
            else:
                side = ref[h, outer, here, :]
            result.append([
                b[h], side, ref[h, kk, pl.ds(r0 + 7, rows), :], ref[h, kk, pl.ds(r0 + 9, rows), :],
                below[h], above[h],
            ])
        return result

    def along_z(b, ends, lane):
        up = [pltpu.roll(v, 1, 1) for v in b]
        down = [pltpu.roll(v, 127, 1) for v in b]
        below = [jnp.where(lane == 0, ends, up[0]), jnp.where(lane == 0, up[0], up[1])]
        above = [jnp.where(lane == 127, down[1], down[0]), jnp.where(lane == 127, ends, down[1])]
        return below, above

    def around_line(own_edge, far, ends):
        b = [line_r[h, pl.ds(1, pairs), :] for h in range(2)]
        below, above = along_z(b, ends, iota((pairs, 128), 1))
        result = []
        for h in range(2):
            before = line_r[h, pl.ds(0, pairs), :]
            after = line_r[h, pl.ds(2, pairs), :]
            side = jnp.where(odd_line, before, after)
            result.append([b[h], side, own_edge[h], far[h], below[h], above[h]])
        return result

    def rows_to(dst, ref, row, first):
        for h in range(2):
            for k in range(pairs):
                dst[h, k : k + 1, :] = ref[h, k + first, pl.ds(row, 1), :]

    def rows_from(src, ref):
        for h in range(2):
            for k in range(pairs):
                ref[h, k + 1, pl.ds(y_halo, 1), :] = src[h, k : k + 1, :]

    def corner_to(dst, ref):
        for h in range(2):
            dst[h : h + 1, :] = ref[h, x_edge, pl.ds(y_edge, 1), :]

    def take_red(ref, xr, yr, dr, outside):
        for h in range(2):
            ref[h, x_halo, 8:top, :] = xr[h]
            ref[h, x_halo, pl.ds(y_halo, 1), :] = dr[h : h + 1, :]
            line_r[h, pl.ds(1, pairs), :] = yr[h]
            line_r[h, pl.ds(x_halo, 1), :] = dr[h : h + 1, :]
            line_r[h, pl.ds(x_far, 1), :] = outside[h]
        rows_from(yr, ref)

    zero_tall = jnp.zeros((ty + 16, 128), F32)

    def clear(kk, _):
        for h in range(2):
            er[h, kk] = zero_tall
            eb[h, kk] = zero_tall
        return 0

    lax.fori_loop(0, pairs + 2, clear, 0)
    sds[...] = jnp.zeros((8, 128), F32)
    for t in range(2):
        dds[t] = jnp.zeros((8, 128), F32)

    def split(ref, k, h):
        low = ref[2 * k, :, pl.ds(128 * h, 128)]
        high = ref[2 * k + 1, :, pl.ds(128 * h, 128)]
        return jnp.where(odd_tile, high, low), jnp.where(odd_tile, low, high)

    def split_eps(k, _):
        for h in range(2):
            er[h, k + 1, 8:top, :], eb[h, k + 1, 8:top, :] = split(raw_e, k, h)
        return 0

    def split_rest(k, _):
        for h in range(2):
            for src, dst in ((raw_k, scr), (raw_s, chg)):
                dst[0, h, k], dst[1, h, k] = split(src, k, h)
        return 0

    raw_in[0].wait()
    loop(pairs, split_eps, 0, 2)
    raw_in[1].wait()
    raw_in[2].wait()
    loop(pairs, split_rest, 0, 2)
    for h in range(2):
        sxs[0, h] = er[h, x_edge, 8:top, :]
        sxs[1, h] = eb[h, x_edge, 8:top, :]
        sxs[2, h] = scr[1, h, x_edge - 1]
        sxs[3, h] = chg[1, h, x_edge - 1]
    rows_to(sys.at[0], er, y_edge, 1)
    rows_to(sys.at[1], er, y_next, 1)
    rows_to(sys.at[2], eb, y_edge, 1)
    rows_to(sys.at[3], scr.at[1], y_edge - 8, 0)
    rows_to(sys.at[4], chg.at[1], y_edge - 8, 0)
    corner_to(sds, er)
    for copy in halo_copies(0):
        copy.start()
    for copy in halo_copies(0):
        copy.wait_recv()
    zero_line = jnp.zeros((1, 128), F32)
    take_red(er, sxr.at[0], syr.at[0], sdr, (zero_line, zero_line))
    for h in range(2):
        eb[h, x_halo, 8:top, :] = sxr[1, h]
    rows_from(syr.at[2], eb)

    def weigh(own, near):
        weights = [0.5 * (own + value) for value in near]
        return weights, sum(weights[1:], weights[0])

    def couple(k, _):
        for colour, mine, other in ((0, er, eb), (1, eb, er)):
            near = around(other, 0.0, colour, k + 1, 0, ty, odd_tile)
            for h in range(2):
                weights, total = weigh(mine[h, k + 1, 8:top, :], near[h])
                for n in range(6):
                    w[colour, n, h, k] = weights[n]
                diag[colour, h, k] = total
        return 0

    loop(pairs, couple, 0, 2)
    near_x = around(er, 0.0, 1, x_halo, 0, ty, odd_tile, x_edge)
    near_y = around_line(sys[0], syr[1], 0.0)
    for h in range(2):
        weights, dx[h] = weigh(eb[h, x_halo, 8:top, :], near_x[h])
        for n in range(6):
            wx[n, h] = weights[n]
        weights, dy[h] = weigh(syr[2, h], near_y[h])
        for n in range(6):
            wy[n, h] = weights[n]

    row = iota((128, 128), 0)
    col = iota((128, 128), 1)
    pz = []
    for h in range(3):
        if h < 2:
            q = col + 128 * h + 1
        else:
            q = jnp.where(col == 0, 0, 257)
        low = q // RATIO
        part = (q - low * RATIO).astype(F32) / RATIO
        pz.append(
            (jnp.where(row == low, 1.0 - part, 0.0) + jnp.where(row == low + 1, part, 0.0)).astype(jnp.bfloat16)
        )

    pltpu.make_async_copy(arrived.at[pl.ds(1, boxes - 1)], arrived.at[pl.ds(1, boxes - 1)], pack_recv).wait()
    row0 = anchors[0, me] + sx * (tx // RATIO)
    first = row0 // 8
    phase = row0 - first * 8
    for t in range(deep // 8):
        holder = jnp.minimum(first + t, boxes - 1)
        slot = lax.rem(me - holder + boxes, boxes)
        extra = arrived[slot, ncols // 2]
        for m in range(ncols // 2):
            part = arrived[slot, m]
            ends = pltpu.roll(extra, 128 - 2 * m, 1) if m > 0 else extra
            even = jnp.where(lane8 < 64, part, ends)
            odd = pltpu.roll(jnp.where(lane8 < 64, ends, part), 64, 1)
            zin[pl.ds((2 * m) * deep + 8 * t, 8), :] = even
            zin[pl.ds((2 * m + 1) * deep + 8 * t, 8), :] = odd
    values = zin[...]
    split_parts = []
    for _ in range(3):
        part = values.astype(jnp.bfloat16)
        split_parts.append(part)
        values = values - part.astype(F32)
    for h in range(3):
        zfine[h] = sum(jnp.dot(part, pz[h], preferred_element_type=F32) for part in reversed(split_parts))

    for h in range(3):
        columns = [zfine[h, pl.ds(c * deep + phase, lines), :] for c in range(ncols)]
        for q in range(ty + 2):
            low, part = q // RATIO, (q % RATIO) / RATIO
            value = columns[low]
            if part > 0:
                value = (1.0 - part) * value + part * columns[low + 1]
            ylines[h, pl.ds((q + 7) * lines, lines), :] = value
    for h in range(3):
        for r in range(nrows):
            xlines[h, r] = ylines[h, pl.ds(r, ty + 16, stride=lines), :]

    def guess(m, _):
        for h in range(3):
            before = xlines[h, jnp.maximum(m - 1, 0)]
            here = xlines[h, m]
            after = xlines[h, m + 1]
            planes = (
                (2 * m, 0.25 * before + 0.75 * here, here),
                (2 * m + 1, 0.75 * here + 0.25 * after, 0.5 * here + 0.5 * after),
            )
            for kk, low, high in planes:
                red = jnp.where(odd_tall, high, low)
                black = jnp.where(odd_tall, low, high)
                if h < 2:
                    ur[h, kk] = red
                    ub[h, kk] = black
                else:
                    uend[0, kk] = red
                    uend[1, kk] = black
        return 0

    loop(tx // RATIO + 1, guess, 0, 2)

    def hyperbolic(value):
        power = value * LOG2E
        plus = jnp.exp2(power - 1.0)
        minus = jnp.exp2(-1.0 - power)
        return plus - minus, plus + minus

    def weighted(weights, near):
        total = weights(0) * near[0]
        for n in (4, 5, 1, 2, 3):
            total = total + weights(n) * near[n]
        return total

    def newton(centre, pull, main, salt):
        sinh, cosh = hyperbolic(centre)
        return centre - (main * centre - pull + salt * sinh) / (main + salt * cosh)

    def square(centre, pull, main, salt):
        g = main * centre - pull + salt * hyperbolic(centre)[0]
        return g * g

    def cells_of(colour, kk, r0, acc, update, residual):
        here = pl.ds(r0, 8)
        own, other = (ur, ub) if colour == 0 else (ub, ur)
        k = kk - 1
        near = around(other, uend[colour, kk, pl.ds(r0 + 8, 8), :], colour, kk, r0, 8, odd8)
        for h in range(2):
            pull = weighted(lambda n: w[colour, n, h, k, here, :], near[h]) + chg[colour, h, k, here, :]
            main = diag[colour, h, k, here, :]
            salt = scr[colour, h, k, here, :]
            value = own[h, kk, pl.ds(r0 + 8, 8), :]
            if update:
                value = newton(value, pull, main, salt)
                own[h, kk, pl.ds(r0 + 8, 8), :] = value
            if residual:
                acc = acc + square(value, pull, main, salt)
        return acc

    inner_pair = 1 + sx
    inner_row = pl.multiple_of(8 * sy, 8)
    edge_row = pl.multiple_of((ty - 8) * (1 - sy), 8)

    def edge(colour, acc, residual):
        for r0 in range(0, ty, 8):
            acc = cells_of(colour, x_edge, r0, acc, True, residual)
        return loop(
            pairs - 1,
            lambda i, acc: cells_of(colour, inner_pair + i, edge_row, acc, True, residual),
            acc, pairs,
        )

    def interior(colour, acc, residual):
        def step(i, acc):
            for s in range(ty // 8 - 1):
                acc = cells_of(colour, inner_pair + i, pl.multiple_of(inner_row + 8 * s, 8), acc, True, residual)
            return acc

        return loop(pairs - 1, step, acc, 5)

    def send_red(t):
        for h in range(2):
            dxs[t, h] = ur[h, x_edge, 8:top, :]
        rows_to(dys.at[t, 0], ur, y_edge, 1)
        rows_to(dys.at[t, 1], ur, y_next, 1)
        corner_to(dds.at[t], ur)
        for copy in halo_copies(1 + t):
            copy.start()

    def take(t):
        for copy in halo_copies(1 + t):
            copy.wait_recv()
        outside = [ur[h, x_far, pl.ds(y_halo, 1), :] for h in range(2)]
        take_red(ur, dxr.at[t], dyr.at[t, 0], ddr.at[t], outside)

    def beside(t):
        near_x = around(ur, uend[1, x_halo, 8:top, :], 1, x_halo, 0, ty, odd_tile, x_edge)
        near_y = around_line(dys[t, 0], dyr[t, 1], line_end[...])
        for h in range(2):
            pull = weighted(lambda n: wx[n, h], near_x[h]) + sxr[3, h]
            ub[h, x_halo, 8:top, :] = newton(ub[h, x_halo, 8:top, :], pull, dx[h], sxr[2, h])
            pull = weighted(lambda n: wy[n, h], near_y[h]) + syr[4, h]
            line_b[h] = newton(line_b[h], pull, dy[h], syr[3, h])
        rows_from(line_b, ub)

    rows_to(line_b, ub, y_halo, 1)
    for k in range(pairs):
        line_end[k : k + 1, :] = uend[1, k + 1, pl.ds(y_halo, 1), :]

    tiles = ty // 8
    rim = min(2, tiles)
    free_row = pl.multiple_of(16 * sy, 8)
    rim_row = pl.multiple_of(8 * (tiles - rim) * (1 - sy), 8)

    def residual_free(i, acc):
        for s in range(tiles - rim):
            acc = cells_of(0, 1 + 2 * sx + i, pl.multiple_of(free_row + 8 * s, 8), acc, False, True)
        return acc

    def residual_rim(i, acc):
        for s in range(rim):
            acc = cells_of(0, 1 + 2 * sx + i, pl.multiple_of(rim_row + 8 * s, 8), acc, False, True)
        return acc

    total = jnp.zeros((8, 128), F32)
    for t in range(2):
        edge(0, total, False)
        send_red(t)
        interior(0, total, False)
        total = interior(1, total, t == 1)
        if t == 1:
            total = loop(pairs - 2, residual_free, total, 6)
        take(t)
        beside(t)
        total = edge(1, total, t == 1)

    for i in range(2):
        for r0 in range(0, ty, 8):
            total = cells_of(0, (pairs - 2) * (1 - sx) + 1 + i, r0, total, False, True)
    sums[group] = loop(pairs - 2, residual_rim, total, 6)
    sum_copies = [
        pltpu.make_async_remote_copy(
            src_ref=sums.at[group], dst_ref=sums.at[group],
            send_sem=ss_sem.at[n], recv_sem=sr_sem.at[n],
            device_id=peer, device_id_type=MESH,
        )
        for n, peer in enumerate(peers)
    ]
    for copy in sum_copies:
        copy.start()

    def join(k, _):
        for h in range(2):
            red = ur[h, k + 1, 8:top, :]
            black = ub[h, k + 1, 8:top, :]
            pot[0, 2 * k, :, pl.ds(128 * h, 128)] = jnp.where(odd_tile, black, red)
            pot[0, 2 * k + 1, :, pl.ds(128 * h, 128)] = jnp.where(odd_tile, red, black)
        return 0

    loop(pairs, join, 0, 2)

    pltpu.make_async_copy(packed.at[pl.ds(1, boxes - 1)], packed.at[pl.ds(1, boxes - 1)], pack_send).wait()
    for slot in range(3):
        for copy in halo_copies(slot):
            copy.wait_send()
    for copy in sum_copies:
        copy.wait()
    squares = jnp.sum(sums[0] + sums[1] + sums[2] + sums[3], keepdims=True)
    norm_out[...] = jnp.sqrt(squares / cells + 1e-06)


def body(coarse, anchors, dielectric, screening, source):
    boxes = lax.axis_size("box")
    _, tx, ty, tz = dielectric.shape
    pairs = tx // 2
    nrows = (tx + 1) // RATIO + 2
    ncols = (ty + 1) // RATIO + 2
    deep = (nrows + 14) // 8 * 8
    lines = (nrows + 7) // 8 * 8
    slabs, gy, gz = coarse.shape
    cells = tx * ty * tz * lax.axis_size("sx") * lax.axis_size("sy")
    any_spec = pl.BlockSpec(memory_space=pl.ANY)
    vmem_spec = pl.BlockSpec(memory_space=pltpu.VMEM)
    dma = pltpu.SemaphoreType.DMA

    def vmem(*shape):
        return pltpu.VMEM(shape, F32)

    def padded():
        return vmem(2, pairs + 2, ty + 16, 128)

    potential, norm = pl.pallas_call(
        functools.partial(kernel, boxes, tx, ty, cells),
        out_shape=(
            jax.ShapeDtypeStruct((1, tx, ty, tz), F32),
            jax.ShapeDtypeStruct((1, 1), F32),
        ),
        in_specs=[any_spec] * 5,
        out_specs=(vmem_spec, vmem_spec),
        scratch_shapes=[
            pltpu.SMEM((3, boxes), jnp.int32),
            vmem(gy, slabs, gz),
            vmem(boxes, ncols // 2 + 1, 8, 128),
            vmem(boxes, ncols // 2 + 1, 8, 128),
            vmem(ncols * deep, 128),
            vmem(3, ncols * deep, 128),
            vmem(3, (ty + 16) * lines, 128),
            vmem(3, nrows, ty + 16, 128),
            vmem(tx, ty, tz),
            vmem(tx, ty, tz),
            vmem(tx, ty, tz),
            padded(),
            padded(),
            vmem(2, 2, pairs, ty, 128),
            vmem(2, 2, pairs, ty, 128),
            vmem(2, 6, 2, pairs, ty, 128),
            vmem(2, 2, pairs, ty, 128),
            padded(),
            padded(),
            padded(),
            vmem(6, 2, ty, 128),
            vmem(2, ty, 128),
            vmem(6, 2, pairs, 128),
            vmem(2, pairs, 128),
            vmem(2, pairs + 4, 128),
            vmem(2, pairs, 128),
            vmem(pairs, 128),
            vmem(4, 2, ty, 128),
            vmem(4, 2, ty, 128),
            vmem(5, 2, pairs, 128),
            vmem(5, 2, pairs, 128),
            vmem(8, 128),
            vmem(8, 128),
            vmem(2, 2, ty, 128),
            vmem(2, 2, ty, 128),
            vmem(2, 2, 2, pairs, 128),
            vmem(2, 2, 2, pairs, 128),
            vmem(2, 8, 128),
            vmem(2, 8, 128),
            vmem(4, 8, 128),
            dma, dma((slabs,)), dma((3,)), dma, dma, dma((9,)), dma((9,)), dma((3,)), dma((3,)),
        ],
        compiler_params=pltpu.CompilerParams(
            collective_id=0, has_side_effects=True, vmem_limit_bytes=52 * 1024 * 1024
        ),
        cost_estimate=pl.CostEstimate(
            flops=200 * tx * ty * tz, bytes_accessed=16 * tx * ty * tz, transcendentals=12 * tx * ty * tz
        ),
    )(*(
        pltpu.with_memory_space_constraint(operand, pltpu.HBM)
        for operand in (anchors.T, coarse, dielectric, screening, source)
    ))
    return potential, norm.reshape(1)


def solution(mesh):
    tile = P("box", "sx", "sy", None)
    return jax.shard_map(
        body,
        mesh=mesh,
        in_specs=(P("box", None, None), P(), tile, tile, tile),
        out_specs=(tile, P("box")),
        check_vma=False,
    )
```

```python
import functools

import jax
import jax.numpy as jnp
from jax import lax
from jax.experimental import pallas as pl
from jax.experimental.pallas import tpu as pltpu
from jax.sharding import PartitionSpec as P

RATIO = 4
LOG2E = 1.4426950408889634
MESH = pl.DeviceIdType.MESH
F32 = jnp.float32


def iota(shape, dim):
    return lax.broadcasted_iota(jnp.int32, shape, dim)


def loop(count, step, carry, unroll):
    chunks = count // unroll if count > unroll else 0

    def chunk(n, carry):
        for i in range(unroll):
            carry = step(n * unroll + i, carry)
        return carry

    if chunks:
        carry = lax.fori_loop(0, chunks, chunk, carry)
    for i in range(chunks * unroll, count):
        carry = step(i, carry)
    return carry


def kernel(
    boxes, tx, ty, cells,
    anchors_in, coarse, diel, screen, source,
    pot, norm_out,
    anchors, slab, packed, arrived, zin, zfine, ylines, xlines,
    raw_e, raw_k, raw_s, er, eb, scr, chg, w, diag, ur, ub, uend,
    wx, dx, wl, dl, kl, sl, le, lu, lend,
    sxs, sxr, sys, syr, sds, sdr, dxs, dxr, dys, dyr, dds, ddr, sums,
    anchor_sem, slab_sem, raw_sem, pack_send, pack_recv, halo_send, halo_recv, ss_sem, sr_sem,
):
    pairs = tx // 2
    nrows = xlines.shape[1]
    ncols = ty // RATIO + 3
    both = ncols // 2
    slabs = slab.shape[1]
    deep = zin.shape[0] // ncols
    lines = ylines.shape[1] // (ty + 16)
    top = 8 + ty
    me = lax.axis_index("box")
    sx = lax.axis_index("sx")
    sy = lax.axis_index("sy")
    group = 2 * sx + sy
    peers = [{"sx": 1 - sx}, {"sy": 1 - sy}, {"sx": 1 - sx, "sy": 1 - sy}]

    x_edge = pairs + 1 - (pairs - 1) * sx
    x_next = x_edge - 1 + 2 * sx
    x_halo = pairs + 2 - (pairs + 1) * sx
    x_outer = (pairs + 3) * (1 - sx)
    x_far = 1 + (pairs + 1) * sx
    outward = 1 - 2 * sy
    y_edge = top - 1 - (ty - 1) * sy
    own_pairs = pl.ds(2, pairs)
    line_pairs = pl.ds(1, pairs + 2)

    anchor_in = pltpu.make_async_copy(anchors_in, anchors, anchor_sem)
    slab_in = [
        pltpu.make_async_copy(coarse.at[r], slab.at[:, r, :], slab_sem.at[r]) for r in range(slabs)
    ]
    raw_in = [
        pltpu.make_async_copy(src.at[0], dst, raw_sem.at[n])
        for n, (src, dst) in enumerate(((diel, raw_e), (screen, raw_k), (source, raw_s)))
    ]
    anchor_in.start()
    for copy in slab_in:
        copy.start()

    barrier = pltpu.get_barrier_semaphore()

    def greet(d, _):
        pl.semaphore_signal(
            barrier, inc=1, device_id={"box": lax.rem(me + d, boxes)}, device_id_type=MESH
        )
        return 0

    lax.fori_loop(1, boxes, greet, 0)
    for peer in peers:
        pl.semaphore_signal(barrier, inc=1, device_id=peer, device_id_type=MESH)
    for copy in raw_in:
        copy.start()

    lane8 = iota((8, 128), 1)

    def window(d):
        b = lax.rem(me + d, boxes)
        y0 = anchors[1, b] + sy * (ty // RATIO - 1)
        z0 = anchors[2, b]
        to_even = lax.rem(128 - z0, 128)
        to_odd = lax.rem(192 - z0, 128)
        parts = []
        last = pltpu.roll(slab[y0 + 2 * both], to_odd, 1)
        extra = jnp.where(lane8 < 64, pltpu.roll(last, 4 * both, 1), last)
        for m in range(both):
            even = pltpu.roll(slab[y0 + 2 * m], to_even, 1)
            odd = pltpu.roll(slab[y0 + 2 * m + 1], to_odd, 1)
            parts.append(jnp.where(lane8 < 64, even, odd))
            extra = jnp.where(lane8 // 2 == m, pltpu.roll(odd, 2 * m, 1) if m > 0 else odd, extra)
            extra = jnp.where(lane8 // 2 == both + m, pltpu.roll(even, 64 + 2 * (both + m), 1), extra)
        return parts + [extra]

    def pack_window(d, _):
        for m, part in enumerate(window(d + 1)):
            packed[d + 1, m] = part
        return 0

    def send_window(d, _):
        pltpu.make_async_remote_copy(
            src_ref=packed.at[d],
            dst_ref=arrived.at[d],
            send_sem=pack_send,
            recv_sem=pack_recv,
            device_id={"box": lax.rem(me + d, boxes)},
            device_id_type=MESH,
        ).start()
        return 0

    odd_tile = (iota((ty, 128), 0) + iota((ty, 128), 1)) % 2 == 1
    odd_tall = (iota((ty + 16, 128), 0) + iota((ty + 16, 128), 1)) % 2 == 1
    odd8 = (iota((8, 128), 0) + iota((8, 128), 1)) % 2 == 1
    odd_line = (iota((pairs + 2, 128), 1) + y_edge) % 2 == 1

    halo_src = [[sxs, sys, sds], [dxs, dys, dds]]
    halo_dst = [[sxr, syr, sdr], [dxr, dyr, ddr]]

    def halo_copies(slot):
        return [
            pltpu.make_async_remote_copy(
                src_ref=halo_src[slot][n], dst_ref=halo_dst[slot][n],
                send_sem=halo_send.at[3 * slot + n], recv_sem=halo_recv.at[3 * slot + n],
                device_id=peers[n], device_id_type=MESH,
            )
            for n in range(3)
        ]

    def around(ref, ends, colour, kk, r0, rows, odd):
        lane = iota((rows, 128), 1)
        here = pl.ds(r0 + 8, rows)
        b = [ref[h, kk, here, :] for h in range(2)]
        below, above = along_z(b, ends, lane)
        result = []
        for h in range(2):
            before = ref[h, kk - 1, here, :]
            after = ref[h, kk + 1, here, :]
            side = jnp.where(odd, after, before) if colour == 0 else jnp.where(odd, before, after)
            result.append([
                b[h], side, ref[h, kk, pl.ds(r0 + 7, rows), :], ref[h, kk, pl.ds(r0 + 9, rows), :],
                below[h], above[h],
            ])
        return result

    def along_z(b, ends, lane):
        up = [pltpu.roll(v, 1, 1) for v in b]
        down = [pltpu.roll(v, 127, 1) for v in b]
        below = [jnp.where(lane == 0, ends, up[0]), jnp.where(lane == 0, up[0], up[1])]
        above = [jnp.where(lane == 127, down[1], down[0]), jnp.where(lane == 127, ends, down[1])]
        return below, above

    def around_line(mid, near, far, ends, odd_first):
        b = [mid[h, line_pairs, :] for h in range(2)]
        below, above = along_z(b, ends, iota((pairs + 2, 128), 1))
        result = []
        for h in range(2):
            before = mid[h, pl.ds(0, pairs + 2), :]
            after = mid[h, pl.ds(2, pairs + 2), :]
            side = jnp.where(odd_line, after, before) if odd_first else jnp.where(odd_line, before, after)
            result.append([b[h], side, near[h, line_pairs, :], far[h, line_pairs, :], below[h], above[h]])
        return result

    R0, R1, R2, B0, B1, B2, B3 = range(7)
    updates = ((R1, B1, B0, B2, False), (R2, B2, B1, B3, True), (B1, R1, R0, R2, True))

    def rows_to(dst, ref, row, first):
        for h in range(2):
            for k in range(pairs):
                dst[h, k : k + 1, :] = ref[h, k + first, pl.ds(row, 1), :]

    def line_to(dst, ref, row):
        for h in range(2):
            for k in range(pairs + 4):
                dst[h, k : k + 1, :] = ref[h, k, pl.ds(row, 1), :]

    def rows_from(src, first, ref, row):
        for h in range(2):
            for k in range(pairs):
                ref[h, k + 2, pl.ds(row, 1), :] = src[h, k + first : k + first + 1, :]

    zero_tall = jnp.zeros((ty + 16, 128), F32)

    def clear(kk, _):
        for h in range(2):
            er[h, kk] = zero_tall
            eb[h, kk] = zero_tall
        return 0

    lax.fori_loop(0, pairs + 4, clear, 0)
    sds[...] = jnp.zeros((16, 128), F32)
    dds[...] = jnp.zeros((8, 128), F32)

    def split(ref, k, h):
        low = ref[2 * k, :, pl.ds(128 * h, 128)]
        high = ref[2 * k + 1, :, pl.ds(128 * h, 128)]
        return jnp.where(odd_tile, high, low), jnp.where(odd_tile, low, high)

    def split_eps(k, _):
        for h in range(2):
            er[h, k + 2, 8:top, :], eb[h, k + 2, 8:top, :] = split(raw_e, k, h)
        return 0

    def split_rest(k, _):
        for h in range(2):
            for src, dst in ((raw_k, scr), (raw_s, chg)):
                dst[0, h, k], dst[1, h, k] = split(src, k, h)
        return 0

    anchor_in.wait()
    for copy in slab_in:
        copy.wait()
    loop(boxes - 1, pack_window, 0, 4)
    edge_row = pl.multiple_of((ty - 8) * (1 - sy), 8)
    edge_here = pl.ds(edge_row, 8)

    def split_edge(k, _):
        for h in range(2):
            halves = []
            for ref in (raw_e, raw_k, raw_s):
                low = ref[2 * k, edge_here, pl.ds(128 * h, 128)]
                high = ref[2 * k + 1, edge_here, pl.ds(128 * h, 128)]
                halves.append((jnp.where(odd8, high, low), jnp.where(odd8, low, high)))
            er[h, k + 2, pl.ds(edge_row + 8, 8), :], eb[h, k + 2, pl.ds(edge_row + 8, 8), :] = halves[0]
            scr[0, h, k, edge_here, :], scr[1, h, k, edge_here, :] = halves[1]
            chg[0, h, k, edge_here, :], chg[1, h, k, edge_here, :] = halves[2]
        return 0

    for copy in raw_in:
        copy.wait()
    loop(pairs, split_edge, 0, 4)
    for k in (x_edge - 2, x_next - 2):
        split_eps(k, 0)
        split_rest(k, 0)

    inward = [y_edge, y_edge - outward, y_edge - 2 * outward]
    for h in range(2):
        sxs[0, h] = er[h, x_edge, 8:top, :]
        sxs[1, h] = eb[h, x_edge, 8:top, :]
        sxs[2, h] = eb[h, x_next, 8:top, :]
        for colour in range(2):
            sxs[3 + 2 * colour, h] = scr[colour, h, x_edge - 2]
            sxs[4 + 2 * colour, h] = chg[colour, h, x_edge - 2]
        for n, (ref, row) in enumerate(((er, 0), (eb, 0), (eb, 1))):
            sds[2 * n + h : 2 * n + h + 1, :] = ref[h, x_edge, pl.ds(inward[row], 1), :]
        for n, ref in enumerate((scr, chg)):
            sds[6 + 2 * n + h : 7 + 2 * n + h, :] = ref[0, h, x_edge - 2, pl.ds(y_edge - 8, 1), :]
    for n, (ref, row) in enumerate(((er, 0), (er, 1), (eb, 0), (eb, 1), (eb, 2))):
        rows_to(sys.at[n], ref, inward[row], 2)
    for n, (ref, row) in enumerate(((scr.at[0], 0), (chg.at[0], 0), (scr.at[0], 1), (chg.at[0], 1), (scr.at[1], 0), (chg.at[1], 0))):
        rows_to(sys.at[5 + n], ref, inward[row] - 8, 0)
    pl.semaphore_wait(barrier, boxes - 1 + 3)
    for copy in halo_copies(0):
        copy.start()
    lax.fori_loop(1, boxes, send_window, 0)
    for m, part in enumerate(window(0)):
        arrived[0, m] = part

    loop(pairs, split_eps, 0, 2)
    loop(pairs, split_rest, 0, 2)
    def weigh(own, near):
        weights = [0.5 * (own + value) for value in near]
        return weights, sum(weights[1:], weights[0])

    def couple_rows(k, r0, rows, odd):
        here = pl.ds(r0, rows)
        for colour, mine, other in ((0, er, eb), (1, eb, er)):
            near = around(other, 0.0, colour, k + 2, r0, rows, odd)
            for h in range(2):
                weights, total = weigh(mine[h, k + 2, pl.ds(r0 + 8, rows), :], near[h])
                for n in range(6):
                    w[colour, n, h, k, here, :] = weights[n]
                diag[colour, h, k, here, :] = total

    def couple(k, _):
        couple_rows(k, 0, ty, odd_tile)
        return 0

    def couple_edge(k, _):
        couple_rows(k, edge_row, 8, odd8)
        return 0

    loop(pairs, couple, 0, 2)
    row = iota((128, 128), 0)
    col = iota((128, 128), 1)
    pz = []
    for h in range(3):
        if h < 2:
            q = col + 128 * h + 1
        else:
            q = jnp.where(col == 0, 0, 257)
        low = q // RATIO
        part = (q - low * RATIO).astype(F32) / RATIO
        pz.append(
            (jnp.where(row == low, 1.0 - part, 0.0) + jnp.where(row == low + 1, part, 0.0)).astype(jnp.bfloat16)
        )

    pltpu.make_async_copy(arrived.at[pl.ds(1, boxes - 1)], arrived.at[pl.ds(1, boxes - 1)], pack_recv).wait()
    row0 = anchors[0, me] + sx * (tx // RATIO - 1)
    first = row0 // 8
    phase = row0 - first * 8
    for t in range(deep // 8 - 1):
        holder = jnp.minimum(first + t, boxes - 1)
        slot = lax.rem(me - holder + boxes, boxes)
        extra = arrived[slot, both]
        for m in range(both):
            part = arrived[slot, m]
            odd_ends = pltpu.roll(extra, 128 - 2 * m, 1) if m > 0 else extra
            even_ends = pltpu.roll(extra, 64 - 2 * (both + m), 1)
            even = jnp.where(lane8 < 64, part, even_ends)
            odd = pltpu.roll(jnp.where(lane8 < 64, odd_ends, part), 64, 1)
            zin[pl.ds((2 * m) * deep + 8 * t + 8, 8), :] = even
            zin[pl.ds((2 * m + 1) * deep + 8 * t + 8, 8), :] = odd
        last = jnp.where(lane8 < 64, pltpu.roll(extra, 128 - 4 * both, 1), extra)
        zin[pl.ds(2 * both * deep + 8 * t + 8, 8), :] = pltpu.roll(last, 64, 1)
    for c in range(ncols):
        zin[pl.ds(c * deep, 8), :] = jnp.zeros((8, 128), F32)
    values = zin[...]
    split_parts = []
    for _ in range(3):
        part = values.astype(jnp.bfloat16)
        split_parts.append(part)
        values = values - part.astype(F32)
    for h in range(3):
        zfine[h] = sum(jnp.dot(part, pz[h], preferred_element_type=F32) for part in reversed(split_parts))

    for h in range(3):
        columns = [
            zfine[h, pl.ds(jnp.maximum(c + sy, 0) * deep + 7 + phase + sx, lines), :] for c in range(-1, ncols - 1)
        ]
        for q in range(-2, ty + 4):
            low, part = q // RATIO, (q % RATIO) / RATIO
            value = columns[low + 1]
            if part > 0:
                value = (1.0 - part) * value + part * columns[low + 2]
            ylines[h, pl.ds((q + 7) * lines, lines), :] = value
    for h in range(3):
        for r in range(nrows):
            xlines[h, r] = ylines[h, pl.ds(r, ty + 16, stride=lines), :]

    def guess(m, _):
        for h in range(3):
            here = xlines[h, m]
            after = xlines[h, m + 1]
            planes = (
                (2 * m, 0.75 * here + 0.25 * after, 0.5 * here + 0.5 * after),
                (2 * m + 1, 0.25 * here + 0.75 * after, after),
            )
            for kk, low, high in planes:
                red = jnp.where(odd_tall, high, low)
                black = jnp.where(odd_tall, low, high)
                if h < 2:
                    ur[h, kk] = red
                    ub[h, kk] = black
                else:
                    uend[0, kk] = red
                    uend[1, kk] = black
        return 0

    loop(pairs // 2 + 2, guess, 0, 2)

    def hyperbolic(value):
        power = value * LOG2E
        plus = jnp.exp2(power - 1.0)
        minus = jnp.exp2(-1.0 - power)
        return plus - minus, plus + minus

    def weighted(weights, near):
        total = weights(0) * near[0]
        for n in (4, 5, 1, 2, 3):
            total = total + weights(n) * near[n]
        return total

    def newton(centre, pull, main, salt):
        sinh, cosh = hyperbolic(centre)
        return centre - (main * centre - pull + salt * sinh) / (main + salt * cosh)

    def square(centre, pull, main, salt):
        g = main * centre - pull + salt * hyperbolic(centre)[0]
        return g * g

    def cells_of(colour, kk, r0, acc, update, residual):
        here = pl.ds(r0, 8)
        own, other = (ur, ub) if colour == 0 else (ub, ur)
        k = kk - 2
        near = around(other, uend[colour, kk, pl.ds(r0 + 8, 8), :], colour, kk, r0, 8, odd8)
        for h in range(2):
            pull = weighted(lambda n: w[colour, n, h, k, here, :], near[h]) + chg[colour, h, k, here, :]
            main = diag[colour, h, k, here, :]
            salt = scr[colour, h, k, here, :]
            value = own[h, kk, pl.ds(r0 + 8, 8), :]
            if update:
                value = newton(value, pull, main, salt)
                own[h, kk, pl.ds(r0 + 8, 8), :] = value
            if residual:
                acc = acc + square(value, pull, main, salt)
        return acc

    tiles = ty // 8
    rim = min(2, tiles)
    inner_pair = 2 + sx
    free_pair = 2 + 2 * sx
    rim_pair = x_edge - 1 + 2 * sx
    inner_row = pl.multiple_of(8 * sy, 8)
    free_row = pl.multiple_of(16 * sy, 8)
    rim_row = pl.multiple_of(8 * (tiles - rim) * (1 - sy), 8)
    near_row = pl.multiple_of(8 * sy + 8 * (tiles - rim) * (1 - sy), 8)

    def edge(colour, acc, residual):
        for r0 in range(0, ty, 8):
            acc = cells_of(colour, x_edge, r0, acc, True, residual)
        return loop(
            pairs - 1,
            lambda i, acc: cells_of(colour, inner_pair + i, edge_row, acc, True, residual),
            acc, pairs,
        )

    def interior(colour, acc, residual):
        def step(i, acc):
            for s in range(tiles - 1):
                acc = cells_of(colour, inner_pair + i, pl.multiple_of(inner_row + 8 * s, 8), acc, True, residual)
            return acc

        return loop(pairs - 1, step, acc, 5)

    def rim_of(colour, acc):
        for s in range(tiles - 1):
            acc = cells_of(colour, rim_pair, pl.multiple_of(inner_row + 8 * s, 8), acc, True, False)
        if tiles < 2:
            return acc
        return loop(
            pairs - 2, lambda i, acc: cells_of(colour, free_pair + i, near_row, acc, True, False), acc, pairs
        )

    def free(colour, acc, update, residual):
        def step(i, acc):
            for s in range(tiles - rim):
                acc = cells_of(colour, free_pair + i, pl.multiple_of(free_row + 8 * s, 8), acc, update, residual)
            return acc

        return loop(pairs - 2, step, acc, 6)

    def send_red():
        for h in range(2):
            dxs[h] = ur[h, x_edge, 8:top, :]
            dds[h : h + 1, :] = ur[h, x_edge, pl.ds(y_edge, 1), :]
        for n in range(2):
            rows_to(dys.at[n], ur, inward[n], 2)
        for copy in halo_copies(1):
            copy.start()

    def take_red():
        for copy in halo_copies(1):
            copy.wait_recv()
        for h in range(2):
            ur[h, x_halo, 8:top, :] = dxr[h]
            for n in range(2):
                lu[R1 + n, h, own_pairs, :] = dyr[n, h]
            lu[R0, h, own_pairs, :] = dys[0, h]
            lu[R1, h, pl.ds(x_halo, 1), :] = ddr[h : h + 1, :]

    def spread_red():
        for h in range(2):
            ur[h, x_halo, pl.ds(outer_rows[1], 1), :] = lu[R1, h, pl.ds(x_halo, 1), :]
        rows_from(lu.at[R1], 2, ur, outer_rows[1])

    def line_step(i):
        own, mid, near, far, odd_first = updates[i]
        near = around_line(lu.at[mid], lu.at[near], lu.at[far], lend[i, line_pairs, :], odd_first)
        for h in range(2):
            pull = weighted(lambda n: wl[i, n, h], near[h]) + sl[i, h]
            edge_value = lu[own, h, pl.ds(x_far, 1), :]
            lu[own, h, line_pairs, :] = newton(lu[own, h, line_pairs, :], pull, dl[i, h], kl[i, h])
            lu[own, h, pl.ds(x_far, 1), :] = edge_value

    def pair_step(colour):
        mine, other = (ur, ub) if colour == 0 else (ub, ur)
        near = around(other, uend[colour, x_halo, 8:top, :], colour, x_halo, 0, ty, odd_tile)
        for h in range(2):
            pull = weighted(lambda n: wx[colour, n, h], near[h]) + sxr[4 + 2 * colour, h]
            mine[h, x_halo, 8:top, :] = newton(mine[h, x_halo, 8:top, :], pull, dx[colour, h], sxr[3 + 2 * colour, h])

    def black_beside():
        pair_step(1)
        line_step(2)
        rows_from(lu.at[B1], 2, ub, outer_rows[1])

    total = jnp.zeros((8, 128), F32)
    interior(0, total, False)

    for copy in halo_copies(0):
        copy.wait_recv()
    outer_rows = [y_edge + n * outward for n in range(4)]
    for h in range(2):
        er[h, x_halo, 8:top, :] = sxr[0, h]
        eb[h, x_halo, 8:top, :] = sxr[1, h]
        eb[h, x_outer, 8:top, :] = sxr[2, h]
        for n, (ref, row) in enumerate(((er, 1), (eb, 1), (eb, 2))):
            ref[h, x_halo, pl.ds(outer_rows[row], 1), :] = sdr[2 * n + h : 2 * n + h + 1, :]
    for n, (ref, row) in enumerate(((er, 1), (er, 2), (eb, 1), (eb, 2), (eb, 3))):
        rows_from(syr.at[n], 0, ref, outer_rows[row])
    for n in range(3):
        for h in range(2):
            kl[n, h, pl.ds(1, pairs), :] = syr[5 + 2 * n, h]
            sl[n, h, pl.ds(1, pairs), :] = syr[6 + 2 * n, h]
    for h in range(2):
        kl[0, h, pl.ds(x_halo - 1, 1), :] = sdr[6 + h : 7 + h, :]
        sl[0, h, pl.ds(x_halo - 1, 1), :] = sdr[8 + h : 9 + h, :]
    for n in range(7):
        line_to(le.at[n], er if n < 3 else eb, outer_rows[n if n < 3 else n - 3])
    loop(pairs, couple_edge, 0, 5)
    couple(x_edge - 2, 0)
    for colour, mine, other in ((0, er, eb), (1, eb, er)):
        near = around(other, 0.0, colour, x_halo, 0, ty, odd_tile)
        for h in range(2):
            weights, dx[colour, h] = weigh(mine[h, x_halo, 8:top, :], near[h])
            for n in range(6):
                wx[colour, n, h] = weights[n]
    for i, (own, mid, near, far, odd_first) in enumerate(updates):
        near = around_line(le.at[mid], le.at[near], le.at[far], 0.0, odd_first)
        for h in range(2):
            weights, dl[i, h] = weigh(le[own, h, line_pairs, :], near[h])
            for n in range(6):
                wl[i, n, h] = weights[n]

    for n in range(7):
        line_to(lu.at[n], ur if n < 3 else ub, outer_rows[n if n < 3 else n - 3])
    for i, (colour, row) in enumerate(((0, 1), (0, 2), (1, 1))):
        for k in range(pairs + 4):
            lend[i, k : k + 1, :] = uend[colour, k, pl.ds(outer_rows[row], 1), :]
    edge(0, total, False)
    pair_step(0)
    line_step(0)
    line_step(1)
    spread_red()
    line_to(lu.at[R0], ur, y_edge)
    black_beside()
    edge(1, total, False)
    rim_of(1, total)
    edge(0, total, False)
    send_red()
    free(1, total, True, False)
    interior(0, total, False)
    total = interior(1, total, True)
    total = free(0, total, False, True)
    take_red()
    spread_red()
    black_beside()
    total = edge(1, total, True)

    def residual_rim(i, acc):
        for s in range(rim):
            acc = cells_of(0, free_pair + i, pl.multiple_of(rim_row + 8 * s, 8), acc, False, True)
        return acc

    for i in range(2):
        for r0 in range(0, ty, 8):
            total = cells_of(0, (pairs - 2) * (1 - sx) + 2 + i, r0, total, False, True)
    sums[group] = loop(pairs - 2, residual_rim, total, 6)
    sum_copies = [
        pltpu.make_async_remote_copy(
            src_ref=sums.at[group], dst_ref=sums.at[group],
            send_sem=ss_sem.at[n], recv_sem=sr_sem.at[n],
            device_id=peer, device_id_type=MESH,
        )
        for n, peer in enumerate(peers)
    ]
    for copy in sum_copies:
        copy.start()

    def join(k, _):
        for h in range(2):
            red = ur[h, k + 2, 8:top, :]
            black = ub[h, k + 2, 8:top, :]
            pot[0, 2 * k, :, pl.ds(128 * h, 128)] = jnp.where(odd_tile, black, red)
            pot[0, 2 * k + 1, :, pl.ds(128 * h, 128)] = jnp.where(odd_tile, red, black)
        return 0

    loop(pairs, join, 0, 2)

    pltpu.make_async_copy(packed.at[pl.ds(1, boxes - 1)], packed.at[pl.ds(1, boxes - 1)], pack_send).wait()
    for slot in range(2):
        for copy in halo_copies(slot):
            copy.wait_send()
    for copy in sum_copies:
        copy.wait()
    squares = jnp.sum(sums[0] + sums[1] + sums[2] + sums[3], keepdims=True)
    norm_out[...] = jnp.sqrt(squares / cells + 1e-06)


def body(coarse, anchors, dielectric, screening, source):
    boxes = lax.axis_size("box")
    _, tx, ty, tz = dielectric.shape
    pairs = tx // 2
    nrows = pairs // 2 + 3
    ncols = ty // RATIO + 3
    deep = (nrows + 14) // 8 * 8 + 8
    lines = (nrows + 7) // 8 * 8
    slabs, gy, gz = coarse.shape
    cells = tx * ty * tz * lax.axis_size("sx") * lax.axis_size("sy")
    any_spec = pl.BlockSpec(memory_space=pl.ANY)
    vmem_spec = pl.BlockSpec(memory_space=pltpu.VMEM)
    dma = pltpu.SemaphoreType.DMA

    def vmem(*shape):
        return pltpu.VMEM(shape, F32)

    def padded():
        return vmem(2, pairs + 4, ty + 16, 128)

    potential, norm = pl.pallas_call(
        functools.partial(kernel, boxes, tx, ty, cells),
        out_shape=(
            jax.ShapeDtypeStruct((1, tx, ty, tz), F32),
            jax.ShapeDtypeStruct((1, 1), F32),
        ),
        in_specs=[any_spec] * 5,
        out_specs=(vmem_spec, vmem_spec),
        scratch_shapes=[
            pltpu.SMEM((3, boxes), jnp.int32),
            vmem(gy, slabs, gz),
            vmem(boxes, ncols // 2 + 1, 8, 128),
            vmem(boxes, ncols // 2 + 1, 8, 128),
            vmem(ncols * deep, 128),
            vmem(3, ncols * deep, 128),
            vmem(3, (ty + 16) * lines, 128),
            vmem(3, nrows, ty + 16, 128),
            vmem(tx, ty, tz),
            vmem(tx, ty, tz),
            vmem(tx, ty, tz),
            padded(),
            padded(),
            vmem(2, 2, pairs, ty, 128),
            vmem(2, 2, pairs, ty, 128),
            vmem(2, 6, 2, pairs, ty, 128),
            vmem(2, 2, pairs, ty, 128),
            padded(),
            padded(),
            padded(),
            vmem(2, 6, 2, ty, 128),
            vmem(2, 2, ty, 128),
            vmem(3, 6, 2, pairs + 2, 128),
            vmem(3, 2, pairs + 2, 128),
            vmem(3, 2, pairs + 2, 128),
            vmem(3, 2, pairs + 2, 128),
            vmem(7, 2, pairs + 4, 128),
            vmem(7, 2, pairs + 4, 128),
            vmem(3, pairs + 4, 128),
            vmem(7, 2, ty, 128),
            vmem(7, 2, ty, 128),
            vmem(11, 2, pairs, 128),
            vmem(11, 2, pairs, 128),
            vmem(16, 128),
            vmem(16, 128),
            vmem(2, ty, 128),
            vmem(2, ty, 128),
            vmem(2, 2, pairs, 128),
            vmem(2, 2, pairs, 128),
            vmem(8, 128),
            vmem(8, 128),
            vmem(4, 8, 128),
            dma, dma((slabs,)), dma((3,)), dma, dma, dma((6,)), dma((6,)), dma((3,)), dma((3,)),
        ],
        compiler_params=pltpu.CompilerParams(
            collective_id=0, has_side_effects=True, vmem_limit_bytes=52 * 1024 * 1024
        ),
        cost_estimate=pl.CostEstimate(
            flops=200 * tx * ty * tz, bytes_accessed=16 * tx * ty * tz, transcendentals=12 * tx * ty * tz
        ),
    )(*(
        pltpu.with_memory_space_constraint(operand, pltpu.HBM)
        for operand in (anchors.T, coarse, dielectric, screening, source)
    ))
    return potential, norm.reshape(1)


def solution(mesh):
    tile = P("box", "sx", "sy", None)
    return jax.shard_map(
        body,
        mesh=mesh,
        in_specs=(P("box", None, None), P(), tile, tile, tile),
        out_specs=(tile, P("box")),
        check_vma=False,
    )
```

```python
import functools

import jax
import jax.numpy as jnp
from jax import lax
from jax.experimental import pallas as pl
from jax.experimental.pallas import tpu as pltpu
from jax.sharding import PartitionSpec as P

RATIO = 4
LOG2E = 1.4426950408889634
MESH = pl.DeviceIdType.MESH
F32 = jnp.float32


def iota(shape, dim):
    return lax.broadcasted_iota(jnp.int32, shape, dim)


def loop(count, step, carry, unroll):
    chunks = count // unroll if count > unroll else 0

    def chunk(n, carry):
        for i in range(unroll):
            carry = step(n * unroll + i, carry)
        return carry

    if chunks:
        carry = lax.fori_loop(0, chunks, chunk, carry)
    for i in range(chunks * unroll, count):
        carry = step(i, carry)
    return carry


def kernel(
    boxes, tx, ty, cells,
    anchors_in, coarse, diel, screen, source,
    pot, norm_out,
    anchors, slab, packed, arrived, zin, zfine, ylines, xlines,
    raw_e, raw_k, raw_s, er, eb, scr, chg, w, diag, ur, ub, uend,
    wx, dx, wl, dl, kl, sl, le, lu, lend,
    sxs, sxr, sys, syr, sds, sdr, dxs, dxr, dys, dyr, dds, ddr, sums,
    anchor_sem, slab_sem, raw_sem, pack_send, pack_recv, halo_send, halo_recv, ss_sem, sr_sem,
):
    pairs = tx // 2
    nrows = xlines.shape[1]
    ncols = ty // RATIO + 3
    both = ncols // 2
    slabs = slab.shape[1]
    deep = zin.shape[0] // ncols
    lines = ylines.shape[1] // (ty + 16)
    top = 8 + ty
    me = lax.axis_index("box")
    sx = lax.axis_index("sx")
    sy = lax.axis_index("sy")
    group = 2 * sx + sy
    peers = [{"sx": 1 - sx}, {"sy": 1 - sy}, {"sx": 1 - sx, "sy": 1 - sy}]

    x_edge = pairs + 1 - (pairs - 1) * sx
    x_next = x_edge - 1 + 2 * sx
    x_halo = pairs + 2 - (pairs + 1) * sx
    x_outer = (pairs + 3) * (1 - sx)
    x_far = 1 + (pairs + 1) * sx
    outward = 1 - 2 * sy
    y_edge = top - 1 - (ty - 1) * sy
    own_pairs = pl.ds(2, pairs)
    line_pairs = pl.ds(1, pairs + 2)

    anchor_in = pltpu.make_async_copy(anchors_in, anchors, anchor_sem)
    slab_in = [
        pltpu.make_async_copy(coarse.at[r], slab.at[:, r, :], slab_sem.at[r]) for r in range(slabs)
    ]
    raw_in = [
        pltpu.make_async_copy(src.at[0], dst, raw_sem.at[n])
        for n, (src, dst) in enumerate(((diel, raw_e), (screen, raw_k), (source, raw_s)))
    ]
    anchor_in.start()
    for copy in slab_in:
        copy.start()

    barrier = pltpu.get_barrier_semaphore()

    def greet(d, _):
        pl.semaphore_signal(
            barrier, inc=1, device_id={"box": lax.rem(me + d, boxes)}, device_id_type=MESH
        )
        return 0

    lax.fori_loop(1, boxes, greet, 0)
    for peer in peers:
        pl.semaphore_signal(barrier, inc=1, device_id=peer, device_id_type=MESH)
    for copy in raw_in:
        copy.start()

    lane8 = iota((8, 128), 1)

    def window(d):
        b = lax.rem(me + d, boxes)
        y0 = anchors[1, b] + sy * (ty // RATIO - 1)
        z0 = anchors[2, b]
        to_even = lax.rem(128 - z0, 128)
        to_odd = lax.rem(192 - z0, 128)
        parts = []
        last = pltpu.roll(slab[y0 + 2 * both], to_odd, 1)
        extra = jnp.where(lane8 < 64, pltpu.roll(last, 4 * both, 1), last)
        for m in range(both):
            even = pltpu.roll(slab[y0 + 2 * m], to_even, 1)
            odd = pltpu.roll(slab[y0 + 2 * m + 1], to_odd, 1)
            parts.append(jnp.where(lane8 < 64, even, odd))
            extra = jnp.where(lane8 // 2 == m, pltpu.roll(odd, 2 * m, 1) if m > 0 else odd, extra)
            extra = jnp.where(lane8 // 2 == both + m, pltpu.roll(even, 64 + 2 * (both + m), 1), extra)
        return parts + [extra]

    def pack_window(d, _):
        for m, part in enumerate(window(d + 1)):
            packed[d + 1, m] = part
        return 0

    def send_window(d, _):
        pltpu.make_async_remote_copy(
            src_ref=packed.at[d],
            dst_ref=arrived.at[d],
            send_sem=pack_send,
            recv_sem=pack_recv,
            device_id={"box": lax.rem(me + d, boxes)},
            device_id_type=MESH,
        ).start()
        return 0

    odd_tile = (iota((ty, 128), 0) + iota((ty, 128), 1)) % 2 == 1
    odd_tall = (iota((ty + 16, 128), 0) + iota((ty + 16, 128), 1)) % 2 == 1
    odd8 = (iota((8, 128), 0) + iota((8, 128), 1)) % 2 == 1
    odd_line = (iota((pairs + 2, 128), 1) + y_edge) % 2 == 1

    halo_src = [[sxs, sys, sds], [dxs, dys, dds]]
    halo_dst = [[sxr, syr, sdr], [dxr, dyr, ddr]]

    def halo_copies(slot):
        return [
            pltpu.make_async_remote_copy(
                src_ref=halo_src[slot][n], dst_ref=halo_dst[slot][n],
                send_sem=halo_send.at[3 * slot + n], recv_sem=halo_recv.at[3 * slot + n],
                device_id=peers[n], device_id_type=MESH,
            )
            for n in range(3)
        ]

    def around(ref, ends, colour, kk, r0, rows, odd):
        lane = iota((rows, 128), 1)
        here = pl.ds(r0 + 8, rows)
        b = [ref[h, kk, here, :] for h in range(2)]
        below, above = along_z(b, ends, lane)
        result = []
        for h in range(2):
            before = ref[h, kk - 1, here, :]
            after = ref[h, kk + 1, here, :]
            side = jnp.where(odd, after, before) if colour == 0 else jnp.where(odd, before, after)
            result.append([
                b[h], side, ref[h, kk, pl.ds(r0 + 7, rows), :], ref[h, kk, pl.ds(r0 + 9, rows), :],
                below[h], above[h],
            ])
        return result

    def along_z(b, ends, lane):
        up = [pltpu.roll(v, 1, 1) for v in b]
        down = [pltpu.roll(v, 127, 1) for v in b]
        below = [jnp.where(lane == 0, ends, up[0]), jnp.where(lane == 0, up[0], up[1])]
        above = [jnp.where(lane == 127, down[1], down[0]), jnp.where(lane == 127, ends, down[1])]
        return below, above

    def around_line(mid, near, far, ends, odd_first):
        b = [mid[h, line_pairs, :] for h in range(2)]
        below, above = along_z(b, ends, iota((pairs + 2, 128), 1))
        result = []
        for h in range(2):
            before = mid[h, pl.ds(0, pairs + 2), :]
            after = mid[h, pl.ds(2, pairs + 2), :]
            side = jnp.where(odd_line, after, before) if odd_first else jnp.where(odd_line, before, after)
            result.append([b[h], side, near[h, line_pairs, :], far[h, line_pairs, :], below[h], above[h]])
        return result

    R0, R1, R2, B0, B1, B2, B3 = range(7)
    updates = ((R1, B1, B0, B2, False), (R2, B2, B1, B3, True), (B1, R1, R0, R2, True))

    def rows_to(dst, ref, row, first):
        for h in range(2):
            for k in range(pairs):
                dst[h, k : k + 1, :] = ref[h, k + first, pl.ds(row, 1), :]

    def line_to(dst, ref, row):
        for h in range(2):
            for k in range(pairs + 4):
                dst[h, k : k + 1, :] = ref[h, k, pl.ds(row, 1), :]

    def rows_from(src, first, ref, row):
        for h in range(2):
            for k in range(pairs):
                ref[h, k + 2, pl.ds(row, 1), :] = src[h, k + first : k + first + 1, :]

    zero_tall = jnp.zeros((ty + 16, 128), F32)

    def clear(kk, _):
        for h in range(2):
            er[h, kk] = zero_tall
            eb[h, kk] = zero_tall
        return 0

    lax.fori_loop(0, pairs + 4, clear, 0)
    sds[...] = jnp.zeros((16, 128), F32)
    for n in range(7):
        for h in range(2):
            le[n, h] = jnp.zeros((pairs + 4, 128), F32)
    dds[...] = jnp.zeros((8, 128), F32)

    def split(ref, k, h):
        low = ref[2 * k, :, pl.ds(128 * h, 128)]
        high = ref[2 * k + 1, :, pl.ds(128 * h, 128)]
        return jnp.where(odd_tile, high, low), jnp.where(odd_tile, low, high)

    def split_eps(k, _):
        for h in range(2):
            er[h, k + 2, 8:top, :], eb[h, k + 2, 8:top, :] = split(raw_e, k, h)
        return 0

    def split_rest(k, _):
        for h in range(2):
            for src, dst in ((raw_k, scr), (raw_s, chg)):
                dst[0, h, k], dst[1, h, k] = split(src, k, h)
        return 0

    anchor_in.wait()
    for copy in slab_in:
        copy.wait()
    loop(boxes - 1, pack_window, 0, 4)
    edge_row = pl.multiple_of((ty - 8) * (1 - sy), 8)
    edge_here = pl.ds(edge_row, 8)

    def split_edge(k, _):
        for h in range(2):
            halves = []
            for ref in (raw_e, raw_k, raw_s):
                low = ref[2 * k, edge_here, pl.ds(128 * h, 128)]
                high = ref[2 * k + 1, edge_here, pl.ds(128 * h, 128)]
                halves.append((jnp.where(odd8, high, low), jnp.where(odd8, low, high)))
            er[h, k + 2, pl.ds(edge_row + 8, 8), :], eb[h, k + 2, pl.ds(edge_row + 8, 8), :] = halves[0]
            scr[0, h, k, edge_here, :], scr[1, h, k, edge_here, :] = halves[1]
            chg[0, h, k, edge_here, :], chg[1, h, k, edge_here, :] = halves[2]
        return 0

    for copy in raw_in:
        copy.wait()
    loop(pairs, split_edge, 0, 4)
    for k in (x_edge - 2, x_next - 2):
        split_eps(k, 0)
        split_rest(k, 0)

    inward = [y_edge, y_edge - outward, y_edge - 2 * outward]
    for h in range(2):
        sxs[0, h] = er[h, x_edge, 8:top, :]
        sxs[1, h] = eb[h, x_edge, 8:top, :]
        sxs[2, h] = eb[h, x_next, 8:top, :]
        for colour in range(2):
            sxs[3 + 2 * colour, h] = scr[colour, h, x_edge - 2]
            sxs[4 + 2 * colour, h] = chg[colour, h, x_edge - 2]
        for n, (ref, row) in enumerate(((er, 0), (eb, 0), (eb, 1))):
            sds[2 * n + h : 2 * n + h + 1, :] = ref[h, x_edge, pl.ds(inward[row], 1), :]
        for n, ref in enumerate((scr, chg)):
            sds[6 + 2 * n + h : 7 + 2 * n + h, :] = ref[0, h, x_edge - 2, pl.ds(y_edge - 8, 1), :]
    for n, (ref, row) in enumerate(((er, 0), (er, 1), (eb, 0), (eb, 1), (eb, 2))):
        rows_to(sys.at[n], ref, inward[row], 2)
    for n, (ref, row) in enumerate(((scr.at[0], 0), (chg.at[0], 0), (scr.at[0], 1), (chg.at[0], 1), (scr.at[1], 0), (chg.at[1], 0))):
        rows_to(sys.at[5 + n], ref, inward[row] - 8, 0)
    pl.semaphore_wait(barrier, boxes - 1 + 3)
    for copy in halo_copies(0):
        copy.start()
    lax.fori_loop(1, boxes, send_window, 0)
    for m, part in enumerate(window(0)):
        arrived[0, m] = part

    loop(pairs, split_eps, 0, 2)
    loop(pairs, split_rest, 0, 2)
    def weigh(own, near):
        weights = [0.5 * (own + value) for value in near]
        return weights, sum(weights[1:], weights[0])

    def couple_rows(k, r0, rows, odd):
        here = pl.ds(r0, rows)
        for colour, mine, other in ((0, er, eb), (1, eb, er)):
            near = around(other, 0.0, colour, k + 2, r0, rows, odd)
            for h in range(2):
                weights, total = weigh(mine[h, k + 2, pl.ds(r0 + 8, rows), :], near[h])
                for n in range(6):
                    w[colour, n, h, k, here, :] = weights[n]
                diag[colour, h, k, here, :] = total

    def couple(k, _):
        couple_rows(k, 0, ty, odd_tile)
        return 0

    def couple_edge(k, _):
        couple_rows(k, edge_row, 8, odd8)
        return 0

    loop(pairs, couple, 0, 2)
    row = iota((128, 128), 0)
    col = iota((128, 128), 1)
    pz = []
    for h in range(3):
        if h < 2:
            q = col + 128 * h + 1
        else:
            q = jnp.where(col == 0, 0, 257)
        low = q // RATIO
        part = (q - low * RATIO).astype(F32) / RATIO
        pz.append(
            (jnp.where(row == low, 1.0 - part, 0.0) + jnp.where(row == low + 1, part, 0.0)).astype(jnp.bfloat16)
        )

    pz_all = jnp.concatenate([jnp.concatenate(pz, axis=1)] * 3, axis=0)

    pltpu.make_async_copy(arrived.at[pl.ds(1, boxes - 1)], arrived.at[pl.ds(1, boxes - 1)], pack_recv).wait()
    row0 = anchors[0, me] + sx * (tx // RATIO - 1)
    first = row0 // 8
    phase = row0 - first * 8
    for t in range(deep // 8 - 1):
        holder = jnp.minimum(first + t, boxes - 1)
        slot = lax.rem(me - holder + boxes, boxes)
        extra = arrived[slot, both]
        for m in range(both):
            part = arrived[slot, m]
            odd_ends = pltpu.roll(extra, 128 - 2 * m, 1) if m > 0 else extra
            even_ends = pltpu.roll(extra, 64 - 2 * (both + m), 1)
            even = jnp.where(lane8 < 64, part, even_ends)
            odd = pltpu.roll(jnp.where(lane8 < 64, odd_ends, part), 64, 1)
            zin[pl.ds((2 * m) * deep + 8 * t + 8, 8), :] = even
            zin[pl.ds((2 * m + 1) * deep + 8 * t + 8, 8), :] = odd
        last = jnp.where(lane8 < 64, pltpu.roll(extra, 128 - 4 * both, 1), extra)
        zin[pl.ds(2 * both * deep + 8 * t + 8, 8), :] = pltpu.roll(last, 64, 1)
    for c in range(ncols):
        zin[pl.ds(c * deep, 8), :] = jnp.zeros((8, 128), F32)
    values = zin[...]
    split_parts = []
    for _ in range(3):
        part = values.astype(jnp.bfloat16)
        split_parts.append(part)
        values = values - part.astype(F32)
    product = jnp.dot(jnp.concatenate(split_parts, axis=1), pz_all, preferred_element_type=F32)
    for h in range(3):
        zfine[h] = product[:, 128 * h : 128 * h + 128]

    for h in range(3):
        columns = [
            zfine[h, pl.ds(jnp.maximum(c + sy, 0) * deep + 7 + phase + sx, lines), :] for c in range(-1, ncols - 1)
        ]
        for q in range(-2, ty + 4):
            low, part = q // RATIO, (q % RATIO) / RATIO
            value = columns[low + 1]
            if part > 0:
                value = (1.0 - part) * value + part * columns[low + 2]
            ylines[h, pl.ds((q + 7) * lines, lines), :] = value
    for h in range(3):
        for r in range(nrows):
            xlines[h, r] = ylines[h, pl.ds(r, ty + 16, stride=lines), :]

    def guess(m, _):
        for h in range(3):
            here = xlines[h, m]
            after = xlines[h, m + 1]
            planes = (
                (2 * m, 0.75 * here + 0.25 * after, 0.5 * here + 0.5 * after),
                (2 * m + 1, 0.25 * here + 0.75 * after, after),
            )
            for kk, low, high in planes:
                red = jnp.where(odd_tall, high, low)
                black = jnp.where(odd_tall, low, high)
                if h < 2:
                    ur[h, kk] = red
                    ub[h, kk] = black
                else:
                    uend[0, kk] = red
                    uend[1, kk] = black
        return 0

    loop(pairs // 2 + 2, guess, 0, 2)

    def hyperbolic(value):
        power = value * LOG2E
        plus = jnp.exp2(power - 1.0)
        minus = jnp.exp2(-1.0 - power)
        return plus - minus, plus + minus

    def weighted(weights, near):
        total = weights(0) * near[0]
        for n in (4, 5, 1, 2, 3):
            total = total + weights(n) * near[n]
        return total

    def newton(centre, pull, main, salt):
        sinh, cosh = hyperbolic(centre)
        return centre - (main * centre - pull + salt * sinh) / (main + salt * cosh)

    def square(centre, pull, main, salt):
        g = main * centre - pull + salt * hyperbolic(centre)[0]
        return g * g

    def cells_of(colour, kk, r0, acc, update, residual):
        here = pl.ds(r0, 8)
        own, other = (ur, ub) if colour == 0 else (ub, ur)
        k = kk - 2
        near = around(other, uend[colour, kk, pl.ds(r0 + 8, 8), :], colour, kk, r0, 8, odd8)
        for h in range(2):
            pull = weighted(lambda n: w[colour, n, h, k, here, :], near[h]) + chg[colour, h, k, here, :]
            main = diag[colour, h, k, here, :]
            salt = scr[colour, h, k, here, :]
            value = own[h, kk, pl.ds(r0 + 8, 8), :]
            if update:
                value = newton(value, pull, main, salt)
                own[h, kk, pl.ds(r0 + 8, 8), :] = value
            if residual:
                acc = acc + square(value, pull, main, salt)
        return acc

    tiles = ty // 8
    rim = min(2, tiles)
    inner_pair = 2 + sx
    free_pair = 2 + 2 * sx
    rim_pair = x_edge - 1 + 2 * sx
    inner_row = pl.multiple_of(8 * sy, 8)
    free_row = pl.multiple_of(16 * sy, 8)
    rim_row = pl.multiple_of(8 * (tiles - rim) * (1 - sy), 8)
    near_row = pl.multiple_of(8 * sy + 8 * (tiles - rim) * (1 - sy), 8)

    def edge(colour, acc, residual):
        for r0 in range(0, ty, 8):
            acc = cells_of(colour, x_edge, r0, acc, True, residual)
        return loop(
            pairs - 1,
            lambda i, acc: cells_of(colour, inner_pair + i, edge_row, acc, True, residual),
            acc, pairs,
        )

    def interior(colour, acc, residual):
        def step(i, acc):
            for s in range(tiles - 1):
                acc = cells_of(colour, inner_pair + i, pl.multiple_of(inner_row + 8 * s, 8), acc, True, residual)
            return acc

        return loop(pairs - 1, step, acc, 5)

    def rim_of(colour, acc):
        for s in range(tiles - 1):
            acc = cells_of(colour, rim_pair, pl.multiple_of(inner_row + 8 * s, 8), acc, True, False)
        if tiles < 2:
            return acc
        return loop(
            pairs - 2, lambda i, acc: cells_of(colour, free_pair + i, near_row, acc, True, False), acc, pairs
        )

    def free(colour, acc, update, residual):
        def step(i, acc):
            for s in range(tiles - rim):
                acc = cells_of(colour, free_pair + i, pl.multiple_of(free_row + 8 * s, 8), acc, update, residual)
            return acc

        return loop(pairs - 2, step, acc, 6)

    def send_red():
        for h in range(2):
            dxs[h] = ur[h, x_edge, 8:top, :]
            dds[h : h + 1, :] = ur[h, x_edge, pl.ds(y_edge, 1), :]
        for n in range(2):
            rows_to(dys.at[n], ur, inward[n], 2)
        for copy in halo_copies(1):
            copy.start()

    def take_red():
        for copy in halo_copies(1):
            copy.wait_recv()
        for h in range(2):
            ur[h, x_halo, 8:top, :] = dxr[h]
            for n in range(2):
                lu[R1 + n, h, own_pairs, :] = dyr[n, h]
            lu[R0, h, own_pairs, :] = dys[0, h]
            lu[R1, h, pl.ds(x_halo, 1), :] = ddr[h : h + 1, :]

    def spread_red():
        for h in range(2):
            ur[h, x_halo, pl.ds(outer_rows[1], 1), :] = lu[R1, h, pl.ds(x_halo, 1), :]
        rows_from(lu.at[R1], 2, ur, outer_rows[1])

    def line_step(i):
        own, mid, near, far, odd_first = updates[i]
        near = around_line(lu.at[mid], lu.at[near], lu.at[far], lend[i, line_pairs, :], odd_first)
        for h in range(2):
            pull = weighted(lambda n: wl[i, n, h], near[h]) + sl[i, h]
            edge_value = lu[own, h, pl.ds(x_far, 1), :]
            lu[own, h, line_pairs, :] = newton(lu[own, h, line_pairs, :], pull, dl[i, h], kl[i, h])
            lu[own, h, pl.ds(x_far, 1), :] = edge_value

    def pair_step(colour):
        mine, other = (ur, ub) if colour == 0 else (ub, ur)
        near = around(other, uend[colour, x_halo, 8:top, :], colour, x_halo, 0, ty, odd_tile)
        for h in range(2):
            pull = weighted(lambda n: wx[colour, n, h], near[h]) + sxr[4 + 2 * colour, h]
            mine[h, x_halo, 8:top, :] = newton(mine[h, x_halo, 8:top, :], pull, dx[colour, h], sxr[3 + 2 * colour, h])

    def black_beside():
        pair_step(1)
        line_step(2)
        rows_from(lu.at[B1], 2, ub, outer_rows[1])

    total = jnp.zeros((8, 128), F32)
    interior(0, total, False)

    for copy in halo_copies(0):
        copy.wait_recv()
    outer_rows = [y_edge + n * outward for n in range(4)]
    for h in range(2):
        er[h, x_halo, 8:top, :] = sxr[0, h]
        eb[h, x_halo, 8:top, :] = sxr[1, h]
        eb[h, x_outer, 8:top, :] = sxr[2, h]
        for n, (ref, row) in enumerate(((er, 1), (eb, 1), (eb, 2))):
            ref[h, x_halo, pl.ds(outer_rows[row], 1), :] = sdr[2 * n + h : 2 * n + h + 1, :]
    rows_from(syr.at[0], 0, er, outer_rows[1])
    rows_from(syr.at[2], 0, eb, outer_rows[1])
    for n in range(3):
        for h in range(2):
            kl[n, h, pl.ds(1, pairs), :] = syr[5 + 2 * n, h]
            sl[n, h, pl.ds(1, pairs), :] = syr[6 + 2 * n, h]
    for h in range(2):
        kl[0, h, pl.ds(x_halo - 1, 1), :] = sdr[6 + h : 7 + h, :]
        sl[0, h, pl.ds(x_halo - 1, 1), :] = sdr[8 + h : 9 + h, :]
    for n, ref in ((R0, sys.at[0]), (R1, syr.at[0]), (R2, syr.at[1]), (B0, sys.at[2]), (B1, syr.at[2]), (B2, syr.at[3]), (B3, syr.at[4])):
        for h in range(2):
            le[n, h, own_pairs, :] = ref[h]
    for h in range(2):
        for n, line in enumerate((R1, B1, B2)):
            le[line, h, pl.ds(x_halo, 1), :] = sdr[2 * n + h : 2 * n + h + 1, :]
        le[B0, h, pl.ds(x_halo, 1), :] = sxr[1, h, pl.ds(y_edge - 8, 1), :]
    loop(pairs, couple_edge, 0, 5)
    couple(x_edge - 2, 0)
    for colour, mine, other in ((0, er, eb), (1, eb, er)):
        near = around(other, 0.0, colour, x_halo, 0, ty, odd_tile)
        for h in range(2):
            weights, dx[colour, h] = weigh(mine[h, x_halo, 8:top, :], near[h])
            for n in range(6):
                wx[colour, n, h] = weights[n]
    for i, (own, mid, near, far, odd_first) in enumerate(updates):
        near = around_line(le.at[mid], le.at[near], le.at[far], 0.0, odd_first)
        for h in range(2):
            weights, dl[i, h] = weigh(le[own, h, line_pairs, :], near[h])
            for n in range(6):
                wl[i, n, h] = weights[n]

    for n in range(1, 7):
        line_to(lu.at[n], ur if n < 3 else ub, outer_rows[n if n < 3 else n - 3])
    for i, (colour, row) in enumerate(((0, 1), (0, 2), (1, 1))):
        for k in range(pairs + 4):
            lend[i, k : k + 1, :] = uend[colour, k, pl.ds(outer_rows[row], 1), :]
    edge(0, total, False)
    pair_step(0)
    line_step(0)
    line_step(1)
    spread_red()
    line_to(lu.at[R0], ur, y_edge)
    black_beside()
    edge(1, total, False)
    rim_of(1, total)
    edge(0, total, False)
    send_red()
    free(1, total, True, False)
    interior(0, total, False)
    total = interior(1, total, True)
    total = free(0, total, False, True)
    take_red()
    spread_red()
    black_beside()
    total = edge(1, total, True)

    def residual_rim(i, acc):
        for s in range(rim):
            acc = cells_of(0, free_pair + i, pl.multiple_of(rim_row + 8 * s, 8), acc, False, True)
        return acc

    for i in range(2):
        for r0 in range(0, ty, 8):
            total = cells_of(0, (pairs - 2) * (1 - sx) + 2 + i, r0, total, False, True)
    sums[group] = loop(pairs - 2, residual_rim, total, 6)
    sum_copies = [
        pltpu.make_async_remote_copy(
            src_ref=sums.at[group], dst_ref=sums.at[group],
            send_sem=ss_sem.at[n], recv_sem=sr_sem.at[n],
            device_id=peer, device_id_type=MESH,
        )
        for n, peer in enumerate(peers)
    ]
    for copy in sum_copies:
        copy.start()

    def join(k, _):
        for h in range(2):
            red = ur[h, k + 2, 8:top, :]
            black = ub[h, k + 2, 8:top, :]
            pot[0, 2 * k, :, pl.ds(128 * h, 128)] = jnp.where(odd_tile, black, red)
            pot[0, 2 * k + 1, :, pl.ds(128 * h, 128)] = jnp.where(odd_tile, red, black)
        return 0

    loop(pairs, join, 0, 2)

    pltpu.make_async_copy(packed.at[pl.ds(1, boxes - 1)], packed.at[pl.ds(1, boxes - 1)], pack_send).wait()
    for slot in range(2):
        for copy in halo_copies(slot):
            copy.wait_send()
    for copy in sum_copies:
        copy.wait()
    squares = jnp.sum(sums[0] + sums[1] + sums[2] + sums[3], keepdims=True)
    norm_out[...] = jnp.sqrt(squares / cells + 1e-06)


def body(coarse, anchors, dielectric, screening, source):
    boxes = lax.axis_size("box")
    _, tx, ty, tz = dielectric.shape
    pairs = tx // 2
    nrows = pairs // 2 + 3
    ncols = ty // RATIO + 3
    deep = (nrows + 14) // 8 * 8 + 8
    lines = (nrows + 7) // 8 * 8
    slabs, gy, gz = coarse.shape
    cells = tx * ty * tz * lax.axis_size("sx") * lax.axis_size("sy")
    any_spec = pl.BlockSpec(memory_space=pl.ANY)
    vmem_spec = pl.BlockSpec(memory_space=pltpu.VMEM)
    dma = pltpu.SemaphoreType.DMA

    def vmem(*shape):
        return pltpu.VMEM(shape, F32)

    def padded():
        return vmem(2, pairs + 4, ty + 16, 128)

    potential, norm = pl.pallas_call(
        functools.partial(kernel, boxes, tx, ty, cells),
        out_shape=(
            jax.ShapeDtypeStruct((1, tx, ty, tz), F32),
            jax.ShapeDtypeStruct((1, 1), F32),
        ),
        in_specs=[any_spec] * 5,
        out_specs=(vmem_spec, vmem_spec),
        scratch_shapes=[
            pltpu.SMEM((3, boxes), jnp.int32),
            vmem(gy, slabs, gz),
            vmem(boxes, ncols // 2 + 1, 8, 128),
            vmem(boxes, ncols // 2 + 1, 8, 128),
            vmem(ncols * deep, 128),
            vmem(3, ncols * deep, 128),
            vmem(3, (ty + 16) * lines, 128),
            vmem(3, nrows, ty + 16, 128),
            vmem(tx, ty, tz),
            vmem(tx, ty, tz),
            vmem(tx, ty, tz),
            padded(),
            padded(),
            vmem(2, 2, pairs, ty, 128),
            vmem(2, 2, pairs, ty, 128),
            vmem(2, 6, 2, pairs, ty, 128),
            vmem(2, 2, pairs, ty, 128),
            padded(),
            padded(),
            padded(),
            vmem(2, 6, 2, ty, 128),
            vmem(2, 2, ty, 128),
            vmem(3, 6, 2, pairs + 2, 128),
            vmem(3, 2, pairs + 2, 128),
            vmem(3, 2, pairs + 2, 128),
            vmem(3, 2, pairs + 2, 128),
            vmem(7, 2, pairs + 4, 128),
            vmem(7, 2, pairs + 4, 128),
            vmem(3, pairs + 4, 128),
            vmem(7, 2, ty, 128),
            vmem(7, 2, ty, 128),
            vmem(11, 2, pairs, 128),
            vmem(11, 2, pairs, 128),
            vmem(16, 128),
            vmem(16, 128),
            vmem(2, ty, 128),
            vmem(2, ty, 128),
            vmem(2, 2, pairs, 128),
            vmem(2, 2, pairs, 128),
            vmem(8, 128),
            vmem(8, 128),
            vmem(4, 8, 128),
            dma, dma((slabs,)), dma((3,)), dma, dma, dma((6,)), dma((6,)), dma((3,)), dma((3,)),
        ],
        compiler_params=pltpu.CompilerParams(
            collective_id=0, has_side_effects=True, vmem_limit_bytes=52 * 1024 * 1024
        ),
        cost_estimate=pl.CostEstimate(
            flops=200 * tx * ty * tz, bytes_accessed=16 * tx * ty * tz, transcendentals=12 * tx * ty * tz
        ),
    )(*(
        pltpu.with_memory_space_constraint(operand, pltpu.HBM)
        for operand in (anchors.T, coarse, dielectric, screening, source)
    ))
    return potential, norm.reshape(1)


def solution(mesh):
    tile = P("box", "sx", "sy", None)
    return jax.shard_map(
        body,
        mesh=mesh,
        in_specs=(P("box", None, None), P(), tile, tile, tile),
        out_specs=(tile, P("box")),
        check_vma=False,
    )
```

```python
import functools

import jax
import jax.numpy as jnp
from jax import lax
from jax.experimental import pallas as pl
from jax.experimental.pallas import tpu as pltpu
from jax.sharding import PartitionSpec as P

RATIO = 4
LOG2E = 1.4426950408889634
MESH = pl.DeviceIdType.MESH
F32 = jnp.float32


def iota(shape, dim):
    return lax.broadcasted_iota(jnp.int32, shape, dim)


def loop(count, step, carry, unroll):
    chunks = count // unroll if count > unroll else 0

    def chunk(n, carry):
        for i in range(unroll):
            carry = step(n * unroll + i, carry)
        return carry

    if chunks:
        carry = lax.fori_loop(0, chunks, chunk, carry)
    for i in range(chunks * unroll, count):
        carry = step(i, carry)
    return carry


def kernel(
    boxes, tx, ty, cells,
    anchors_in, coarse, diel, screen, source,
    pot, norm_out,
    anchors, slab, packed, arrived, zin, zfine, ylines, xlines,
    raw_e, raw_k, raw_s, er, eb, scr, chg, w, diag, ur, ub, uend,
    wx, dx, wl, dl, kl, sl, le, lu, lend,
    sxs, sxr, sys, syr, sds, sdr, dxs, dxr, dys, dyr, dds, ddr, sums,
    anchor_sem, slab_sem, raw_sem, pack_send, pack_recv, halo_send, halo_recv, ss_sem, sr_sem,
):
    pairs = tx // 2
    nrows = xlines.shape[1]
    ncols = ty // RATIO + 3
    both = ncols // 2
    slabs = slab.shape[1]
    deep = zin.shape[0] // ncols
    lines = ylines.shape[1] // (ty + 16)
    top = 8 + ty
    me = lax.axis_index("box")
    sx = lax.axis_index("sx")
    sy = lax.axis_index("sy")
    group = 2 * sx + sy
    peers = [{"sx": 1 - sx}, {"sy": 1 - sy}, {"sx": 1 - sx, "sy": 1 - sy}]

    x_edge = pairs + 1 - (pairs - 1) * sx
    x_next = x_edge - 1 + 2 * sx
    x_halo = pairs + 2 - (pairs + 1) * sx
    x_outer = (pairs + 3) * (1 - sx)
    x_far = 1 + (pairs + 1) * sx
    outward = 1 - 2 * sy
    y_edge = top - 1 - (ty - 1) * sy
    own_pairs = pl.ds(2, pairs)
    line_pairs = pl.ds(1, pairs + 2)

    anchor_in = pltpu.make_async_copy(anchors_in, anchors, anchor_sem)
    slab_in = [
        pltpu.make_async_copy(coarse.at[r], slab.at[:, r, :], slab_sem.at[r]) for r in range(slabs)
    ]
    raw_in = [
        pltpu.make_async_copy(src.at[0], dst, raw_sem.at[n])
        for n, (src, dst) in enumerate(((diel, raw_e), (screen, raw_k), (source, raw_s)))
    ]
    anchor_in.start()
    for copy in slab_in:
        copy.start()

    barrier = pltpu.get_barrier_semaphore()

    def greet(d, _):
        pl.semaphore_signal(
            barrier, inc=1, device_id={"box": lax.rem(me + d, boxes)}, device_id_type=MESH
        )
        return 0

    lax.fori_loop(1, boxes, greet, 0)
    for peer in peers:
        pl.semaphore_signal(barrier, inc=1, device_id=peer, device_id_type=MESH)
    for copy in raw_in:
        copy.start()

    lane8 = iota((8, 128), 1)

    def window(d):
        b = lax.rem(me + d, boxes)
        y0 = anchors[1, b] + sy * (ty // RATIO - 1)
        z0 = anchors[2, b]
        to_even = lax.rem(128 - z0, 128)
        to_odd = lax.rem(192 - z0, 128)
        parts = []
        last = pltpu.roll(slab[y0 + 2 * both], to_odd, 1)
        extra = jnp.where(lane8 < 64, pltpu.roll(last, 4 * both, 1), last)
        for m in range(both):
            even = pltpu.roll(slab[y0 + 2 * m], to_even, 1)
            odd = pltpu.roll(slab[y0 + 2 * m + 1], to_odd, 1)
            parts.append(jnp.where(lane8 < 64, even, odd))
            extra = jnp.where(lane8 // 2 == m, pltpu.roll(odd, 2 * m, 1) if m > 0 else odd, extra)
            extra = jnp.where(lane8 // 2 == both + m, pltpu.roll(even, 64 + 2 * (both + m), 1), extra)
        return parts + [extra]

    def pack_window(d, _):
        for m, part in enumerate(window(d + 1)):
            packed[d + 1, m] = part
        return 0

    def send_window(d, _):
        pltpu.make_async_remote_copy(
            src_ref=packed.at[d],
            dst_ref=arrived.at[d],
            send_sem=pack_send,
            recv_sem=pack_recv,
            device_id={"box": lax.rem(me + d, boxes)},
            device_id_type=MESH,
        ).start()
        return 0

    odd_tile = (iota((ty, 128), 0) + iota((ty, 128), 1)) % 2 == 1
    odd_tall = (iota((ty + 16, 128), 0) + iota((ty + 16, 128), 1)) % 2 == 1
    odd8 = (iota((8, 128), 0) + iota((8, 128), 1)) % 2 == 1
    odd_line = (iota((pairs + 2, 128), 1) + y_edge) % 2 == 1

    halo_src = [[sxs, sys, sds], [dxs, dys, dds]]
    halo_dst = [[sxr, syr, sdr], [dxr, dyr, ddr]]

    def halo_copies(slot):
        return [
            pltpu.make_async_remote_copy(
                src_ref=halo_src[slot][n], dst_ref=halo_dst[slot][n],
                send_sem=halo_send.at[3 * slot + n], recv_sem=halo_recv.at[3 * slot + n],
                device_id=peers[n], device_id_type=MESH,
            )
            for n in range(3)
        ]

    def around(ref, ends, colour, kk, r0, rows, odd):
        lane = iota((rows, 128), 1)
        here = pl.ds(r0 + 8, rows)
        b = [ref[h, kk, here, :] for h in range(2)]
        below, above = along_z(b, ends, lane)
        result = []
        for h in range(2):
            before = ref[h, kk - 1, here, :]
            after = ref[h, kk + 1, here, :]
            side = jnp.where(odd, after, before) if colour == 0 else jnp.where(odd, before, after)
            result.append([
                b[h], side, ref[h, kk, pl.ds(r0 + 7, rows), :], ref[h, kk, pl.ds(r0 + 9, rows), :],
                below[h], above[h],
            ])
        return result

    def along_z(b, ends, lane):
        up = [pltpu.roll(v, 1, 1) for v in b]
        down = [pltpu.roll(v, 127, 1) for v in b]
        below = [jnp.where(lane == 0, ends, up[0]), jnp.where(lane == 0, up[0], up[1])]
        above = [jnp.where(lane == 127, down[1], down[0]), jnp.where(lane == 127, ends, down[1])]
        return below, above

    def around_line(mid, near, far, ends, odd_first):
        b = [mid[h, line_pairs, :] for h in range(2)]
        below, above = along_z(b, ends, iota((pairs + 2, 128), 1))
        result = []
        for h in range(2):
            before = mid[h, pl.ds(0, pairs + 2), :]
            after = mid[h, pl.ds(2, pairs + 2), :]
            side = jnp.where(odd_line, after, before) if odd_first else jnp.where(odd_line, before, after)
            result.append([b[h], side, near[h, line_pairs, :], far[h, line_pairs, :], below[h], above[h]])
        return result

    R0, R1, R2, B0, B1, B2, B3 = range(7)
    updates = ((R1, B1, B0, B2, False), (R2, B2, B1, B3, True), (B1, R1, R0, R2, True))

    def rows_to(dst, ref, row, first):
        for h in range(2):
            for k in range(pairs):
                dst[h, k : k + 1, :] = ref[h, k + first, pl.ds(row, 1), :]

    def line_to(dst, ref, row):
        for h in range(2):
            for k in range(pairs + 4):
                dst[h, k : k + 1, :] = ref[h, k, pl.ds(row, 1), :]

    def rows_from(src, first, ref, row):
        for h in range(2):
            for k in range(pairs):
                ref[h, k + 2, pl.ds(row, 1), :] = src[h, k + first : k + first + 1, :]

    zero_tall = jnp.zeros((ty + 16, 128), F32)

    def clear(kk, _):
        for h in range(2):
            er[h, kk] = zero_tall
            eb[h, kk] = zero_tall
        return 0

    lax.fori_loop(0, pairs + 4, clear, 0)
    sds[...] = jnp.zeros((16, 128), F32)
    for n in range(7):
        for h in range(2):
            le[n, h] = jnp.zeros((pairs + 12, 128), F32)
    dds[...] = jnp.zeros((8, 128), F32)

    def split(ref, k, h):
        low = ref[2 * k, :, pl.ds(128 * h, 128)]
        high = ref[2 * k + 1, :, pl.ds(128 * h, 128)]
        return jnp.where(odd_tile, high, low), jnp.where(odd_tile, low, high)

    def split_eps(k, _):
        for h in range(2):
            er[h, k + 2, 8:top, :], eb[h, k + 2, 8:top, :] = split(raw_e, k, h)
        return 0

    def split_rest(k, _):
        for h in range(2):
            for src, dst in ((raw_k, scr), (raw_s, chg)):
                dst[0, h, k], dst[1, h, k] = split(src, k, h)
        return 0

    anchor_in.wait()
    for copy in slab_in:
        copy.wait()
    loop(boxes - 1, pack_window, 0, 4)
    edge_row = pl.multiple_of((ty - 8) * (1 - sy), 8)
    edge_here = pl.ds(edge_row, 8)

    def split_edge(k, _):
        for h in range(2):
            halves = []
            for ref in (raw_e, raw_k, raw_s):
                low = ref[2 * k, edge_here, pl.ds(128 * h, 128)]
                high = ref[2 * k + 1, edge_here, pl.ds(128 * h, 128)]
                halves.append((jnp.where(odd8, high, low), jnp.where(odd8, low, high)))
            er[h, k + 2, pl.ds(edge_row + 8, 8), :], eb[h, k + 2, pl.ds(edge_row + 8, 8), :] = halves[0]
            scr[0, h, k, edge_here, :], scr[1, h, k, edge_here, :] = halves[1]
            chg[0, h, k, edge_here, :], chg[1, h, k, edge_here, :] = halves[2]
        return 0

    for copy in raw_in:
        copy.wait()
    loop(pairs, split_edge, 0, 4)
    for k in (x_edge - 2, x_next - 2):
        split_eps(k, 0)
        split_rest(k, 0)

    inward = [y_edge, y_edge - outward, y_edge - 2 * outward]
    for h in range(2):
        sxs[0, h] = er[h, x_edge, 8:top, :]
        sxs[1, h] = eb[h, x_edge, 8:top, :]
        sxs[2, h] = eb[h, x_next, 8:top, :]
        for colour in range(2):
            sxs[3 + 2 * colour, h] = scr[colour, h, x_edge - 2]
            sxs[4 + 2 * colour, h] = chg[colour, h, x_edge - 2]
        for n, (ref, row) in enumerate(((er, 0), (eb, 0), (eb, 1))):
            sds[2 * n + h : 2 * n + h + 1, :] = ref[h, x_edge, pl.ds(inward[row], 1), :]
        for n, ref in enumerate((scr, chg)):
            sds[6 + 2 * n + h : 7 + 2 * n + h, :] = ref[0, h, x_edge - 2, pl.ds(y_edge - 8, 1), :]
    for n, (ref, row) in enumerate(((er, 0), (er, 1), (eb, 0), (eb, 1), (eb, 2))):
        rows_to(sys.at[n], ref, inward[row], 2)
    for n, (ref, row) in enumerate(((scr.at[0], 0), (chg.at[0], 0), (scr.at[0], 1), (chg.at[0], 1), (scr.at[1], 0), (chg.at[1], 0))):
        rows_to(sys.at[5 + n], ref, inward[row] - 8, 0)
    pl.semaphore_wait(barrier, boxes - 1 + 3)
    for copy in halo_copies(0):
        copy.start()
    lax.fori_loop(1, boxes, send_window, 0)
    for m, part in enumerate(window(0)):
        arrived[0, m] = part

    loop(pairs, split_eps, 0, 2)
    loop(pairs, split_rest, 0, 2)
    def weigh(own, near):
        weights = [0.5 * (own + value) for value in near]
        return weights, sum(weights[1:], weights[0])

    def couple_rows(k, r0, rows, odd):
        here = pl.ds(r0, rows)
        for colour, mine, other in ((0, er, eb), (1, eb, er)):
            near = around(other, 0.0, colour, k + 2, r0, rows, odd)
            for h in range(2):
                weights, total = weigh(mine[h, k + 2, pl.ds(r0 + 8, rows), :], near[h])
                for n in range(6):
                    w[colour, n, h, k, here, :] = weights[n]
                diag[colour, h, k, here, :] = total

    def couple(k, _):
        couple_rows(k, 0, ty, odd_tile)
        return 0

    def couple_edge(k, _):
        couple_rows(k, edge_row, 8, odd8)
        return 0

    loop(pairs, couple, 0, 2)
    row = iota((128, 128), 0)
    col = iota((128, 128), 1)
    pz = []
    for h in range(3):
        if h < 2:
            q = col + 128 * h + 1
        else:
            q = jnp.where(col == 0, 0, 257)
        low = q // RATIO
        part = (q - low * RATIO).astype(F32) / RATIO
        pz.append(
            (jnp.where(row == low, 1.0 - part, 0.0) + jnp.where(row == low + 1, part, 0.0)).astype(jnp.bfloat16)
        )

    pz_all = jnp.concatenate([jnp.concatenate(pz, axis=1)] * 3, axis=0)

    pltpu.make_async_copy(arrived.at[pl.ds(1, boxes - 1)], arrived.at[pl.ds(1, boxes - 1)], pack_recv).wait()
    row0 = anchors[0, me] + sx * (tx // RATIO - 1)
    first = row0 // 8
    phase = row0 - first * 8
    for t in range(deep // 8 - 1):
        holder = jnp.minimum(first + t, boxes - 1)
        slot = lax.rem(me - holder + boxes, boxes)
        extra = arrived[slot, both]
        for m in range(both):
            part = arrived[slot, m]
            odd_ends = pltpu.roll(extra, 128 - 2 * m, 1) if m > 0 else extra
            even_ends = pltpu.roll(extra, 64 - 2 * (both + m), 1)
            even = jnp.where(lane8 < 64, part, even_ends)
            odd = pltpu.roll(jnp.where(lane8 < 64, odd_ends, part), 64, 1)
            zin[pl.ds((2 * m) * deep + 8 * t + 8, 8), :] = even
            zin[pl.ds((2 * m + 1) * deep + 8 * t + 8, 8), :] = odd
        last = jnp.where(lane8 < 64, pltpu.roll(extra, 128 - 4 * both, 1), extra)
        zin[pl.ds(2 * both * deep + 8 * t + 8, 8), :] = pltpu.roll(last, 64, 1)
    for c in range(ncols):
        zin[pl.ds(c * deep, 8), :] = jnp.zeros((8, 128), F32)
    values = zin[...]
    split_parts = []
    for _ in range(3):
        part = values.astype(jnp.bfloat16)
        split_parts.append(part)
        values = values - part.astype(F32)
    product = jnp.dot(jnp.concatenate(split_parts, axis=1), pz_all, preferred_element_type=F32)
    for h in range(3):
        zfine[h] = product[:, 128 * h : 128 * h + 128]

    for h in range(3):
        columns = [
            zfine[h, pl.ds(jnp.maximum(c + sy, 0) * deep + 7 + phase + sx, lines), :] for c in range(-1, ncols - 1)
        ]
        for q in range(-2, ty + 4):
            low, part = q // RATIO, (q % RATIO) / RATIO
            value = columns[low + 1]
            if part > 0:
                value = (1.0 - part) * value + part * columns[low + 2]
            ylines[h, pl.ds((q + 7) * lines, lines), :] = value
    for h in range(3):
        for r in range(nrows):
            xlines[h, r] = ylines[h, pl.ds(r, ty + 16, stride=lines), :]

    def guess(m, _):
        for h in range(3):
            here = xlines[h, m]
            after = xlines[h, m + 1]
            planes = (
                (2 * m, 0.75 * here + 0.25 * after, 0.5 * here + 0.5 * after),
                (2 * m + 1, 0.25 * here + 0.75 * after, after),
            )
            for kk, low, high in planes:
                red = jnp.where(odd_tall, high, low)
                black = jnp.where(odd_tall, low, high)
                if h < 2:
                    ur[h, kk] = red
                    ub[h, kk] = black
                else:
                    uend[0, kk] = red
                    uend[1, kk] = black
        return 0

    loop(pairs // 2 + 2, guess, 0, 2)

    def hyperbolic(value):
        power = value * LOG2E
        plus = jnp.exp2(power - 1.0)
        minus = jnp.exp2(-1.0 - power)
        return plus - minus, plus + minus

    def weighted(weights, near):
        total = weights(0) * near[0]
        for n in (4, 5, 1, 2, 3):
            total = total + weights(n) * near[n]
        return total

    def newton(centre, pull, main, salt):
        sinh, cosh = hyperbolic(centre)
        return centre - (main * centre - pull + salt * sinh) / (main + salt * cosh)

    def square(centre, pull, main, salt):
        g = main * centre - pull + salt * hyperbolic(centre)[0]
        return g * g

    def cells_of(colour, kk, r0, acc, update, residual):
        here = pl.ds(r0, 8)
        own, other = (ur, ub) if colour == 0 else (ub, ur)
        k = kk - 2
        near = around(other, uend[colour, kk, pl.ds(r0 + 8, 8), :], colour, kk, r0, 8, odd8)
        for h in range(2):
            pull = weighted(lambda n: w[colour, n, h, k, here, :], near[h]) + chg[colour, h, k, here, :]
            main = diag[colour, h, k, here, :]
            salt = scr[colour, h, k, here, :]
            value = own[h, kk, pl.ds(r0 + 8, 8), :]
            if update:
                value = newton(value, pull, main, salt)
                own[h, kk, pl.ds(r0 + 8, 8), :] = value
            if residual:
                acc = acc + square(value, pull, main, salt)
        return acc

    tiles = ty // 8
    rim = min(2, tiles)
    inner_pair = 2 + sx
    free_pair = 2 + 2 * sx
    rim_pair = x_edge - 1 + 2 * sx
    inner_row = pl.multiple_of(8 * sy, 8)
    free_row = pl.multiple_of(16 * sy, 8)
    rim_row = pl.multiple_of(8 * (tiles - rim) * (1 - sy), 8)
    near_row = pl.multiple_of(8 * sy + 8 * (tiles - rim) * (1 - sy), 8)

    def edge(colour, acc, residual):
        for r0 in range(0, ty, 8):
            acc = cells_of(colour, x_edge, r0, acc, True, residual)
        return loop(
            pairs - 1,
            lambda i, acc: cells_of(colour, inner_pair + i, edge_row, acc, True, residual),
            acc, pairs,
        )

    def interior(colour, acc, residual):
        def step(i, acc):
            for s in range(tiles - 1):
                acc = cells_of(colour, inner_pair + i, pl.multiple_of(inner_row + 8 * s, 8), acc, True, residual)
            return acc

        return loop(pairs - 1, step, acc, 5)

    def rim_of(colour, acc):
        for s in range(tiles - 1):
            acc = cells_of(colour, rim_pair, pl.multiple_of(inner_row + 8 * s, 8), acc, True, False)
        if tiles < 2:
            return acc
        return loop(
            pairs - 2, lambda i, acc: cells_of(colour, free_pair + i, near_row, acc, True, False), acc, pairs
        )

    def free(colour, acc, update, residual):
        def step(i, acc):
            for s in range(tiles - rim):
                acc = cells_of(colour, free_pair + i, pl.multiple_of(free_row + 8 * s, 8), acc, update, residual)
            return acc

        return loop(pairs - 2, step, acc, 6)

    def send_red():
        for h in range(2):
            dxs[h] = ur[h, x_edge, 8:top, :]
            dds[h : h + 1, :] = ur[h, x_edge, pl.ds(y_edge, 1), :]
        for n in range(2):
            rows_to(dys.at[n], ur, inward[n], 2)
        for copy in halo_copies(1):
            copy.start()

    def take_red():
        for copy in halo_copies(1):
            copy.wait_recv()
        for h in range(2):
            ur[h, x_halo, 8:top, :] = dxr[h]
            for n in range(2):
                lu[R1 + n, h, own_pairs, :] = dyr[n, h]
            lu[R0, h, own_pairs, :] = dys[0, h]
            lu[R1, h, pl.ds(x_halo, 1), :] = ddr[h : h + 1, :]

    def spread_red():
        for h in range(2):
            ur[h, x_halo, pl.ds(outer_rows[1], 1), :] = lu[R1, h, pl.ds(x_halo, 1), :]
        rows_from(lu.at[R1], 2, ur, outer_rows[1])

    def line_step(i):
        own, mid, near, far, odd_first = updates[i]
        near = around_line(lu.at[mid], lu.at[near], lu.at[far], lend[i, line_pairs, :], odd_first)
        for h in range(2):
            pull = weighted(lambda n: wl[i, n, h], near[h]) + sl[i, h, 0 : pairs + 2, :]
            edge_value = lu[own, h, pl.ds(x_far, 1), :]
            lu[own, h, line_pairs, :] = newton(lu[own, h, line_pairs, :], pull, dl[i, h], kl[i, h, 0 : pairs + 2, :])
            lu[own, h, pl.ds(x_far, 1), :] = edge_value

    def pair_step(colour):
        mine, other = (ur, ub) if colour == 0 else (ub, ur)
        near = around(other, uend[colour, x_halo, 8:top, :], colour, x_halo, 0, ty, odd_tile)
        for h in range(2):
            pull = weighted(lambda n: wx[colour, n, h], near[h]) + sxr[4 + 2 * colour, h]
            mine[h, x_halo, 8:top, :] = newton(mine[h, x_halo, 8:top, :], pull, dx[colour, h], sxr[3 + 2 * colour, h])

    def black_beside():
        pair_step(1)
        line_step(2)
        rows_from(lu.at[B1], 2, ub, outer_rows[1])

    total = jnp.zeros((8, 128), F32)
    interior(0, total, False)

    for copy in halo_copies(0):
        copy.wait_recv()
    outer_rows = [y_edge + n * outward for n in range(4)]
    for h in range(2):
        er[h, x_halo, 8:top, :] = sxr[0, h]
        eb[h, x_halo, 8:top, :] = sxr[1, h]
        eb[h, x_outer, 8:top, :] = sxr[2, h]
        for n, (ref, row) in enumerate(((er, 1), (eb, 1), (eb, 2))):
            ref[h, x_halo, pl.ds(outer_rows[row], 1), :] = sdr[2 * n + h : 2 * n + h + 1, :]
    rows_from(syr.at[0], 0, er, outer_rows[1])
    rows_from(syr.at[2], 0, eb, outer_rows[1])
    for n in range(3):
        for h in range(2):
            kl[n, h, pl.ds(1, pairs), :] = syr[5 + 2 * n, h]
            sl[n, h, pl.ds(1, pairs), :] = syr[6 + 2 * n, h]
    for h in range(2):
        kl[0, h, pl.ds(x_halo - 1, 1), :] = sdr[6 + h : 7 + h, :]
        sl[0, h, pl.ds(x_halo - 1, 1), :] = sdr[8 + h : 9 + h, :]
    for n, ref in ((R0, sys.at[0]), (R1, syr.at[0]), (R2, syr.at[1]), (B0, sys.at[2]), (B1, syr.at[2]), (B2, syr.at[3]), (B3, syr.at[4])):
        for h in range(2):
            le[n, h, own_pairs, :] = ref[h]
    for h in range(2):
        for n, line in enumerate((R1, B1, B2)):
            le[line, h, pl.ds(x_halo, 1), :] = sdr[2 * n + h : 2 * n + h + 1, :]
        le[B0, h, pl.ds(x_halo, 1), :] = sxr[1, h, pl.ds(y_edge - 8, 1), :]
    loop(pairs, couple_edge, 0, 5)
    couple(x_edge - 2, 0)
    for colour, mine, other in ((0, er, eb), (1, eb, er)):
        near = around(other, 0.0, colour, x_halo, 0, ty, odd_tile)
        for h in range(2):
            weights, dx[colour, h] = weigh(mine[h, x_halo, 8:top, :], near[h])
            for n in range(6):
                wx[colour, n, h] = weights[n]
    for i, (own, mid, near, far, odd_first) in enumerate(updates):
        near = around_line(le.at[mid], le.at[near], le.at[far], 0.0, odd_first)
        for h in range(2):
            weights, dl[i, h] = weigh(le[own, h, line_pairs, :], near[h])
            for n in range(6):
                wl[i, n, h] = weights[n]

    for n in range(1, 7):
        line_to(lu.at[n], ur if n < 3 else ub, outer_rows[n if n < 3 else n - 3])
    for i, (colour, row) in enumerate(((0, 1), (0, 2), (1, 1))):
        for k in range(pairs + 4):
            lend[i, k : k + 1, :] = uend[colour, k, pl.ds(outer_rows[row], 1), :]
    edge(0, total, False)
    pair_step(0)
    line_step(0)
    line_step(1)
    spread_red()
    line_to(lu.at[R0], ur, y_edge)
    black_beside()
    edge(1, total, False)
    rim_of(1, total)
    edge(0, total, False)
    send_red()
    free(1, total, True, False)
    interior(0, total, False)
    total = interior(1, total, True)
    total = free(0, total, False, True)
    take_red()
    spread_red()
    black_beside()
    total = edge(1, total, True)

    def residual_rim(i, acc):
        for s in range(rim):
            acc = cells_of(0, free_pair + i, pl.multiple_of(rim_row + 8 * s, 8), acc, False, True)
        return acc

    for i in range(2):
        for r0 in range(0, ty, 8):
            total = cells_of(0, (pairs - 2) * (1 - sx) + 2 + i, r0, total, False, True)
    sums[group] = loop(pairs - 2, residual_rim, total, 6)
    sum_copies = [
        pltpu.make_async_remote_copy(
            src_ref=sums.at[group], dst_ref=sums.at[group],
            send_sem=ss_sem.at[n], recv_sem=sr_sem.at[n],
            device_id=peer, device_id_type=MESH,
        )
        for n, peer in enumerate(peers)
    ]
    for copy in sum_copies:
        copy.start()

    def join(k, _):
        for h in range(2):
            red = ur[h, k + 2, 8:top, :]
            black = ub[h, k + 2, 8:top, :]
            pot[0, 2 * k, :, pl.ds(128 * h, 128)] = jnp.where(odd_tile, black, red)
            pot[0, 2 * k + 1, :, pl.ds(128 * h, 128)] = jnp.where(odd_tile, red, black)
        return 0

    loop(pairs, join, 0, 2)

    pltpu.make_async_copy(packed.at[pl.ds(1, boxes - 1)], packed.at[pl.ds(1, boxes - 1)], pack_send).wait()
    for slot in range(2):
        for copy in halo_copies(slot):
            copy.wait_send()
    for copy in sum_copies:
        copy.wait()
    squares = jnp.sum(sums[0] + sums[1] + sums[2] + sums[3], keepdims=True)
    norm_out[...] = jnp.sqrt(squares / cells + 1e-06)


def body(coarse, anchors, dielectric, screening, source):
    boxes = lax.axis_size("box")
    _, tx, ty, tz = dielectric.shape
    pairs = tx // 2
    nrows = pairs // 2 + 3
    ncols = ty // RATIO + 3
    deep = (nrows + 14) // 8 * 8 + 8
    lines = (nrows + 7) // 8 * 8
    slabs, gy, gz = coarse.shape
    cells = tx * ty * tz * lax.axis_size("sx") * lax.axis_size("sy")
    any_spec = pl.BlockSpec(memory_space=pl.ANY)
    vmem_spec = pl.BlockSpec(memory_space=pltpu.VMEM)
    dma = pltpu.SemaphoreType.DMA

    def vmem(*shape):
        return pltpu.VMEM(shape, F32)

    def padded():
        return vmem(2, pairs + 5, ty + 16, 128)

    potential, norm = pl.pallas_call(
        functools.partial(kernel, boxes, tx, ty, cells),
        out_shape=(
            jax.ShapeDtypeStruct((1, tx, ty, tz), F32),
            jax.ShapeDtypeStruct((1, 1), F32),
        ),
        in_specs=[any_spec] * 5,
        out_specs=(vmem_spec, vmem_spec),
        scratch_shapes=[
            pltpu.SMEM((3, boxes), jnp.int32),
            vmem(gy, slabs, gz),
            vmem(boxes, ncols // 2 + 1, 8, 128),
            vmem(boxes, ncols // 2 + 1, 8, 128),
            vmem(ncols * deep, 128),
            vmem(3, ncols * deep, 128),
            vmem(3, (ty + 16) * lines, 128),
            vmem(3, nrows, ty + 16, 128),
            vmem(tx, ty, tz),
            vmem(tx, ty, tz),
            vmem(tx, ty, tz),
            padded(),
            padded(),
            vmem(2, 2, pairs + 1, ty, 128),
            vmem(2, 2, pairs + 1, ty, 128),
            vmem(2, 6, 2, pairs, ty, 128),
            vmem(2, 2, pairs, ty, 128),
            padded(),
            padded(),
            padded(),
            vmem(2, 6, 2, ty, 128),
            vmem(2, 2, ty, 128),
            vmem(3, 6, 2, pairs + 2, 128),
            vmem(3, 2, pairs + 2, 128),
            vmem(3, 2, pairs + 12, 128),
            vmem(3, 2, pairs + 12, 128),
            vmem(7, 2, pairs + 12, 128),
            vmem(7, 2, pairs + 12, 128),
            vmem(3, pairs + 12, 128),
            vmem(7, 2, ty, 128),
            vmem(7, 2, ty, 128),
            vmem(11, 2, pairs, 128),
            vmem(11, 2, pairs, 128),
            vmem(16, 128),
            vmem(16, 128),
            vmem(2, ty, 128),
            vmem(2, ty, 128),
            vmem(2, 2, pairs, 128),
            vmem(2, 2, pairs, 128),
            vmem(8, 128),
            vmem(8, 128),
            vmem(4, 8, 128),
            dma, dma((slabs,)), dma((3,)), dma, dma, dma((6,)), dma((6,)), dma((3,)), dma((3,)),
        ],
        compiler_params=pltpu.CompilerParams(
            collective_id=0, has_side_effects=True, vmem_limit_bytes=52 * 1024 * 1024
        ),
        cost_estimate=pl.CostEstimate(
            flops=200 * tx * ty * tz, bytes_accessed=16 * tx * ty * tz, transcendentals=12 * tx * ty * tz
        ),
    )(*(
        pltpu.with_memory_space_constraint(operand, pltpu.HBM)
        for operand in (anchors.T, coarse, dielectric, screening, source)
    ))
    return potential, norm.reshape(1)


def solution(mesh):
    tile = P("box", "sx", "sy", None)
    return jax.shard_map(
        body,
        mesh=mesh,
        in_specs=(P("box", None, None), P(), tile, tile, tile),
        out_specs=(tile, P("box")),
        check_vma=False,
    )
```
